256 devices in a mesh: row: 8 (over x_lo, y), col: 32 (over x_hi, z, core).
Axes of the slice: x: 4 (x_hi: 2, x_lo: 2; x = x_hi * 2 + x_lo), y: 4, z: 8, core: 2. Of those that a mesh axis runs over, the one named last changes fastest.
Arguments:
- images: bfloat16 [2, 256, 512, 512], P(None, 'row', 'col'), may hold values from -6 to 6
- labels: int32 [256, 512], P('row', 'col'), may hold values from 0 to 2
- qkv_weight: bfloat16 [512, 1536], replicated, may hold values from -0.25 to 0.25
- proj_weight: bfloat16 [512, 512], replicated, may hold values from -0.25 to 0.25
- up_weight: bfloat16 [512, 2048], replicated, may hold values from -0.25 to 0.25
- down_weight: bfloat16 [2048, 512], replicated, may hold values from -0.125 to 0.125
- head_scale: float32 [16], replicated, may hold values from 3 to 12
- cross_qkv: bfloat16 [512, 1536], replicated, may hold values from -0.25 to 0.25
- cross_proj: bfloat16 [512, 512], replicated, may hold values from -0.25 to 0.25
- cross_scale: float32 [16], replicated, may hold values from 3 to 12
- diff_up: bfloat16 [512, 1024], replicated, may hold values from -0.25 to 0.25
- diff_down: bfloat16 [1024, 512], replicated, may hold values from -0.1875 to 0.1875
Outputs:
- change: bfloat16 [256, 512, 512], P('row', 'col')
The draws below stay inside these ranges and needn't reach their ends.
All inputs are finite; a program needn't handle non-finite values.
Results may differ from the reference program's by a relative error of at most 0.015.
Values may be sent and summed in bfloat16 or wider, within the bound.
A program may use at most 192 MiB of HBM per device.

```python
import math
import jax
import jax.numpy as jnp
from jax import lax

C = 512
HEADS = 16
HIDDEN_SIZE = 2048
DIFF_HIDDEN = 1024
WIN = 8
SHIFT = 4
H = 256
W = 512


def place_ends(result, rng, least, largest):
    extent = result.shape
    index_at = [jax.random.randint(jax.random.fold_in(rng, axis), (), 0, extent[axis]) for axis in range(len(extent))]
    result = result.at[tuple(index_at)].set(least)
    longest = extent.index(max(extent))
    index_at[longest] = (index_at[longest] + 1) % extent[longest]
    return result.at[tuple(index_at)].set(largest)


def level_of(key, dims, cuts, low, high):
    level = 1.0
    for position, shards_of in cuts:
        steps = jax.random.uniform(jax.random.fold_in(jax.random.fold_in(key, 6), position), (shards_of,), jnp.float32, low / len(cuts), high / len(cuts))
        level = level * jnp.repeat(jnp.exp(steps), dims[position] // shards_of).reshape((-1,) + (1,) * (len(dims) - 1 - position))
    return level


def noise(stream_key, dims, deviation, bound, shards=(), held_as=jnp.bfloat16):
    values = jax.random.normal(stream_key, dims, jnp.float32) * deviation
    if len(shards) > 0:
        values = level_of(stream_key, dims, shards, -0.22, 0.18) * values
    return jnp.clip(values, min=-bound, max=bound).astype(held_as)


def setup_inputs(seed: int = 0) -> dict:
    key_list = jax.random.split(jax.random.key(seed), 13)
    return {
        "images": noise(key_list[0], (2, H, W, C), 1.0, 6.0, ((1, 8), (2, 32))),
        "labels": place_ends(jax.random.randint(key_list[1], (H, W), 0, 3), jax.random.fold_in(key_list[1], 1), 0, 2).astype(jnp.int32),
        "qkv_weight": noise(key_list[2], (C, 3 * C), C ** -0.5, 0.25),
        "proj_weight": noise(key_list[3], (C, C), C ** -0.5, 0.25),
        "up_weight": noise(key_list[4], (C, HIDDEN_SIZE), C ** -0.5, 0.25),
        "down_weight": noise(key_list[5], (HIDDEN_SIZE, C), HIDDEN_SIZE ** -0.5, 0.125),
        "head_scale": jnp.clip(jnp.exp(jax.random.uniform(key_list[6], (HEADS,), jnp.float32, math.log(3.0), math.log(12.0))), 3.0, 12.0),
        "cross_qkv": noise(key_list[7], (C, 3 * C), C ** -0.5, 0.25),
        "cross_proj": noise(key_list[8], (C, C), C ** -0.5, 0.25),
        "cross_scale": jnp.clip(jnp.exp(jax.random.uniform(key_list[9], (HEADS,), jnp.float32, math.log(3.0), math.log(12.0))), 3.0, 12.0),
        "diff_up": noise(key_list[10], (C, DIFF_HIDDEN), C ** -0.5, 0.25),
        "diff_down": noise(key_list[11], (DIFF_HIDDEN, C), DIFF_HIDDEN ** -0.5, 0.1875),
    }


epsilon = 1e-05

def stored(values):
    return lax.optimization_barrier(values.astype(jnp.bfloat16))

def layer_norm(values):
    centre = values - lax.optimization_barrier(jnp.mean(values, axis=-1, keepdims=True))
    spread = lax.optimization_barrier(jnp.mean(centre * centre, axis=-1, keepdims=True))
    return centre * lax.rsqrt(spread + epsilon)

def unit_rows(values):
    length = jnp.sqrt(lax.optimization_barrier(jnp.sum(values * values, axis=-1, keepdims=True)))
    return values / jnp.maximum(length, 1.0)

def to_windows(layout):
    grid_rows, grid_cols, features = layout.shape
    pieces = layout.reshape(grid_rows // WIN, WIN, grid_cols // WIN, WIN, features)
    return pieces.transpose(0, 2, 1, 3, 4).reshape(-1, WIN * WIN, features)

def from_windows(blocks, grid_rows, grid_cols):
    features = blocks.shape[-1]
    pieces = blocks.reshape(grid_rows // WIN, grid_cols // WIN, WIN, WIN, features)
    return pieces.transpose(0, 2, 1, 3, 4).reshape(grid_rows, grid_cols, features)

def window_attend(packed, scales, allowed):
    window_count, token_count, triple = packed.shape
    features = triple // 3
    head_count = scales.shape[0]
    pieces = packed.reshape(window_count, token_count, 3, head_count, features // head_count)
    queries = unit_rows(pieces[:, :, 0].astype(jnp.float32))
    keysets = unit_rows(pieces[:, :, 1].astype(jnp.float32))
    scores = jnp.einsum('wqhe,wkhe->whqk', queries, keysets, precision=lax.Precision.HIGHEST)
    raised = jnp.exp(scores * scales[None, :, None, None])
    if allowed is not None:
        raised = jnp.where(allowed[:, None], raised, 0.0)
    weights = stored(raised / lax.optimization_barrier(jnp.sum(raised, axis=-1, keepdims=True)))
    mixture = jnp.einsum('whqk,wkhe->wqhe', weights.astype(jnp.float32), pieces[:, :, 2].astype(jnp.float32))
    return stored(mixture.reshape(window_count, token_count, features))

def attend_half(layout, grouping, qkv_weight, proj_weight, head_scale):
    date_count, grid_rows, grid_cols, features = layout.shape
    flattened = layout.reshape(-1, features)
    packed = stored(jnp.dot(flattened, qkv_weight, preferred_element_type=jnp.float32))
    packed = packed.reshape(date_count, grid_rows, grid_cols, 3 * features)
    windows = jnp.concatenate([to_windows(packed[member]) for member in range(date_count)], 0)
    region = to_windows(grouping[:, :, None])[:, :, 0]
    allowed = region[:, :, None] == region[:, None, :]
    allowed = jnp.concatenate([allowed] * date_count, 0)
    mixture = window_attend(windows, head_scale, allowed)
    per_date = mixture.shape[0] // date_count
    mixture = jnp.stack([from_windows(mixture[member * per_date:(member + 1) * per_date], grid_rows, grid_cols) for member in range(date_count)])
    projected = jnp.dot(mixture.reshape(-1, features), proj_weight, preferred_element_type=jnp.float32)
    first = stored(flattened.astype(jnp.float32) + layer_norm(projected))
    return first.reshape(layout.shape)

def feed_forward(first, up_weight, down_weight):
    features = first.shape[-1]
    flattened = first.reshape(-1, features)
    inner_act = stored(jax.nn.gelu(jnp.dot(flattened, up_weight, preferred_element_type=jnp.float32)))
    outcome = flattened.astype(jnp.float32) + layer_norm(jnp.dot(inner_act, down_weight, preferred_element_type=jnp.float32))
    return stored(outcome).reshape(first.shape)

def cross_block(restored, cross_qkv, cross_proj, cross_scale, diff_up, diff_down):
    date_count, grid_rows, grid_cols, features = restored.shape
    flattened = restored.reshape(-1, features)
    packed = stored(jnp.dot(flattened, cross_qkv, preferred_element_type=jnp.float32))
    packed = packed.reshape(date_count, grid_rows, grid_cols, 3 * features)
    windows = jnp.concatenate([to_windows(packed[member]) for member in range(date_count)], 1)
    mixture = window_attend(windows, cross_scale, None)
    per_date = WIN * WIN
    mixture = jnp.stack([from_windows(mixture[:, member * per_date:(member + 1) * per_date], grid_rows, grid_cols) for member in range(date_count)])
    projected = jnp.dot(mixture.reshape(-1, features), cross_proj, preferred_element_type=jnp.float32)
    joined = (flattened.astype(jnp.float32) + layer_norm(projected)).reshape(date_count, -1, features)
    contrast = joined[1] - joined[0]
    diff_inner = stored(jax.nn.gelu(jnp.dot(stored(contrast), diff_up, preferred_element_type=jnp.float32)))
    change = contrast + layer_norm(jnp.dot(diff_inner, diff_down, preferred_element_type=jnp.float32))
    return stored(change).reshape(grid_rows, grid_cols, features)

def reference(images, labels, qkv_weight, proj_weight, up_weight, down_weight, head_scale, cross_qkv, cross_proj, cross_scale, diff_up, diff_down):
    shifted = jnp.roll(images, (-SHIFT, -SHIFT), axis=(1, 2))
    anchor_rows = (jnp.arange(H, dtype=jnp.int32) + SHIFT) % H
    anchor_cols = (jnp.arange(W, dtype=jnp.int32) + SHIFT) % W
    grouping = jnp.roll(labels, (-SHIFT, -SHIFT), axis=(0, 1)) * 4
    grouping = grouping + 2 * (anchor_rows < SHIFT).astype(jnp.int32)[:, None] + (anchor_cols < SHIFT).astype(jnp.int32)[None, :]
    band_images = shifted.reshape(2, H // WIN, WIN, W, C).transpose(1, 0, 2, 3, 4)
    band_codes = grouping.reshape(H // WIN, WIN, W)

    def swin_band(band_item):
        first = attend_half(band_item[0], band_item[1], qkv_weight, proj_weight, head_scale)
        return feed_forward(first, up_weight, down_weight)
    second = lax.map(swin_band, (band_images, band_codes))
    second = second.transpose(1, 0, 2, 3, 4).reshape(2, H, W, C)
    restored = jnp.roll(second, (SHIFT, SHIFT), axis=(1, 2))
    band_pairs = restored.reshape(2, H // WIN, WIN, W, C).transpose(1, 0, 2, 3, 4)

    def cross_band(band_pair):
        return cross_block(band_pair, cross_qkv, cross_proj, cross_scale, diff_up, diff_down)
    change = lax.map(cross_band, band_pairs)
    return change.reshape(H, W, C)
```

```python
import functools
import math

import jax
import jax.numpy as jnp
from jax import lax
from jax.experimental import pallas as pl
from jax.experimental.pallas import tpu as pltpu
from jax.sharding import PartitionSpec as P

WIN = 8
SHIFT = 4
HEADS = 16
C = 512
CELL = SHIFT * SHIFT
EPS = 1e-5
LOG2E = math.log2(math.e)
BF = jnp.bfloat16
F32 = jnp.float32
MESH = pl.DeviceIdType.MESH


def dot(a, b):
    return jnp.dot(a, b, preferred_element_type=F32)


def dot_t(a, b):
    return lax.dot_general(a, b, (((1,), (1,)), ((), ())), preferred_element_type=F32)


def iota(shape, dim):
    return lax.broadcasted_iota(jnp.int32, shape, dim)


def norm_rows(v):
    mean = jnp.sum(v, axis=-1, keepdims=True) * (1.0 / C)
    centre = v - mean
    spread = jnp.sum(centre * centre, axis=-1, keepdims=True) * (1.0 / C)
    return centre * lax.rsqrt(spread + EPS)


def gelu_twice(v):
    k = math.sqrt(2.0 / math.pi)
    inner = v * (k + (k * 0.044715) * (v * v))
    return v * (1.0 + jnp.tanh(inner))


def kernel(
    rows, cols, remote,
    img, lab, hs, cs, wqkv_h, wp_h, wu_h, wd_h, cqkv_h, cp_h, du_h, dd_h,
    out,
    im, wqkv, wp, wu, wd, cqkv, cp, du, dd,
    xc, gc, sc, perm, bd, ones4, scale_s, xs, qkv_s, att_s, hid_s, first_s, ob,
    im_sem, w_sem, out_sem, send1, recv1, send2, recv2,
):
    me_r = lax.axis_index("row") if remote else 0
    me_c = lax.axis_index("col") if remote else 0
    up, down = lax.rem(me_r + rows - 1, rows), lax.rem(me_r + 1, rows)
    left, right = lax.rem(me_c + cols - 1, cols), lax.rem(me_c + 1, cols)

    weights = [
        (wqkv_h, wqkv), (wp_h, wp), (wu_h, wu), (wd_h, wd),
        (cqkv_h, cqkv), (cp_h, cp), (du_h, du), (dd_h, dd),
    ]
    loads = [pltpu.make_async_copy(s, d, w_sem.at[n]) for n, (s, d) in enumerate(weights)]
    load_im = pltpu.make_async_copy(img, im, im_sem)
    load_im.start()
    for load in loads:
        load.start()

    if remote:
        barrier = pltpu.get_barrier_semaphore()
        for r, c in ((up, me_c), (down, me_c), (me_r, left), (me_r, right), (up, left), (down, right)):
            pl.semaphore_signal(barrier, inc=1, device_id={"row": r, "col": c}, device_id_type=MESH)

    o = iota((256, 256), 0)
    t = iota((256, 256), 1)
    src = ((o // 64) * 4 + (o // 4) % 4) * 16 + ((o // 16) % 4) * 4 + o % 4
    perm[...] = jnp.where(src == t, 1.0, 0.0).astype(BF)
    bd[...] = jnp.where(o // 32 == t // 32, 1.0, 0.0).astype(BF)
    o4 = iota((512, 128), 0)
    t4 = iota((512, 128), 1)
    ones4[0] = jnp.where((o4 % 256) // 64 == t4 // 32, 1.0, 0.0).astype(BF)
    ones4[1] = jnp.where(o4 // 128 == t4 // 32, 1.0, 0.0).astype(BF)
    lane = iota((8, C), 1) // 32
    for n, ref in ((0, hs), (1, cs)):
        row = jnp.zeros((8, C), F32)
        for h in range(HEADS):
            row = jnp.where(lane == h, ref[h] * LOG2E, row)
        scale_s[n] = row

    tok = iota((512, 32), 0)
    tr = (tok // 64) * 4 + (tok // 4) % 4
    pick_r = jnp.where(tr == iota((512, 32), 1), 1.0, 0.0).astype(BF)
    tok = iota((512, 16), 0)
    tc = ((tok // 16) % 4) * 4 + tok % 4
    by_row = dot(pick_r, lab[...].astype(F32).astype(BF))
    picked = jnp.where(tc == iota((512, 16), 1), by_row, 0.0).astype(BF)
    value = dot(picked, jnp.ones((16, 128), BF)).astype(jnp.int32)
    tok = iota((512, 128), 0)
    gr = (tok // 64) * 4 + (tok // 4) % 4 + me_r * 32
    gcol = ((tok // 16) % 4) * 4 + tok % 4 + me_c * 16
    code = value * 4 + jnp.where(gr < SHIFT, 2, 0) + jnp.where(gcol < SHIFT, 1, 0)
    onehot = jnp.where(code == iota((512, 128), 1), 1.0, 0.0).astype(BF)
    gc[0:8, 0:4] = onehot.reshape(8, 4, CELL, 128)

    load_im.wait()
    for d in range(2):
        for b in range(2):
            block = im[d, 16 * b : 16 * b + 16].reshape(256, C)
            cells = dot(perm[...], block).astype(BF)
            xc[d, 4 * b : 4 * b + 4, 0:4] = cells.reshape(4, 4, CELL, C)

    def send(src, dst, n, r, c, sems, rsems):
        return pltpu.make_async_remote_copy(
            src_ref=src, dst_ref=dst, send_sem=sems.at[n], recv_sem=rsems.at[n],
            device_id={"row": r, "col": c}, device_id_type=MESH,
        )

    if remote:
        pl.semaphore_wait(barrier, 6)
        halo = [
            send(xc.at[:, 1:8, 0], xc.at[:, 1:8, 4], 0, me_r, left, send1, recv1),
            send(gc.at[1:8, 0], gc.at[1:8, 4], 1, me_r, left, send1, recv1),
            send(xc.at[:, 0, 1:4], xc.at[:, 8, 1:4], 2, up, me_c, send1, recv1),
            send(gc.at[0, 1:4], gc.at[8, 1:4], 3, up, me_c, send1, recv1),
            send(xc.at[:, 0, 0], xc.at[:, 8, 4], 4, up, left, send1, recv1),
            send(gc.at[0, 0], gc.at[8, 4], 5, up, left, send1, recv1),
        ]
        for copy in halo:
            copy.start()
        back = [
            send(sc.at[:, 1:7, 4], sc.at[:, 1:7, 0], 0, me_r, right, send2, recv2),
            send(sc.at[:, 7, 4], sc.at[:, 7, 0], 1, me_r, right, send2, recv2),
            send(sc.at[:, 8, 1:4], sc.at[:, 0, 1:4], 2, down, me_c, send2, recv2),
            send(sc.at[:, 8, 4], sc.at[:, 0, 0], 3, down, right, send2, recv2),
        ]

    head_of = iota((1, 128), 1) // 32
    head_mask = [jnp.where(head_of == h, 1.0, 0.0).astype(BF) for h in range(4)]

    def packed_qkv(x, w, scale):
        for n in range(6):
            y = dot(x, w[:, 256 * n : 256 * n + 256]).astype(BF)
            if n < 4:
                ss = dot(y * y, bd[...])
                factor = lax.rsqrt(jnp.maximum(ss, 1.0))
                if n < 2:
                    factor = factor * scale[:, 256 * n : 256 * n + 256]
                y = (y.astype(F32) * factor).astype(BF)
            qkv_s[:, 256 * n : 256 * n + 256] = y

    def stacked(v):
        return jnp.concatenate([v * head_mask[h] for h in range(4)], 0)

    def attend(base, count, ones, mask):
        for g in range(4):
            lanes = slice(128 * g, 128 * g + 128)
            q = qkv_s[base : base + count, lanes]
            k = qkv_s[base : base + count, 512 + 128 * g : 640 + 128 * g]
            v = qkv_s[base : base + count, 1024 + 128 * g : 1152 + 128 * g]
            e = jnp.exp2(dot_t(q, stacked(k))).astype(BF)
            if mask is not None:
                e = e * mask
            o = dot(e, jnp.concatenate([stacked(v), ones], 1))
            att_s[base : base + count, lanes] = (o[:, :128] / o[:, 128:]).astype(BF)

    for n in range(4):
        loads[n].wait()

    def block_step(step, carry):
        if remote:
            @pl.when(step == 1)
            def _():
                halo[0].wait_recv()
                halo[1].wait_recv()

            @pl.when(step == 3)
            def _():
                for copy in halo[2:]:
                    copy.wait_recv()

        spots = []
        for n in range(2):
            p = 2 * step + n
            a = jnp.where(p < 6, lax.rem(p, 3), 3)
            b = jnp.where(p < 6, p // 3, p - 6)
            spots.append((2 * a + 1, 2 * b + 1))
        for n, (i, j) in enumerate(spots):
            for d in range(2):
                for u in range(2):
                    for v in range(2):
                        at = 128 * n + 64 * d + 32 * u + 16 * v
                        xs[at : at + 16] = xc[d, i + u, j + v]
        x = xs[...]
        packed_qkv(x, wqkv, scale_s[0, 0:1])
        for n, (i, j) in enumerate(spots):
            g = jnp.concatenate([gc[i + u, j + v] for u in range(2) for v in range(2)], 0)
            mask = dot_t(g, jnp.concatenate([g] * 4, 0)).astype(BF)
            for d in range(2):
                attend(128 * n + 64 * d, 64, ones4[0, 0:256], mask)
        first = (x.astype(F32) + norm_rows(dot(att_s[...], wp[...]))).astype(BF)
        first_s[...] = first
        for n in range(8):
            h = dot(first, wu[:, 256 * n : 256 * n + 256])
            hid_s[:, 256 * n : 256 * n + 256] = gelu_twice(h).astype(BF)
        second = (first_s[...].astype(F32) + norm_rows(0.5 * dot(hid_s[...], wd[...]))).astype(BF)
        for n, (i, j) in enumerate(spots):
            for d in range(2):
                for u in range(2):
                    for v in range(2):
                        at = 128 * n + 64 * d + 32 * u + 16 * v
                        sc[d, i + u, j + v] = second[at : at + 16]
        if remote:
            @pl.when(step == 2)
            def _():
                back[0].start()

            @pl.when(step == 3)
            def _():
                for copy in back[1:]:
                    copy.start()
        return carry

    lax.fori_loop(0, 4, block_step, 0)
    for n in range(4, 8):
        loads[n].wait()

    def cross_step(step, carry):
        band = lax.rem(step + 1, 4)
        if remote:
            @pl.when(step == 0)
            def _():
                back[0].wait_recv()

            @pl.when(step == 2)
            def _():
                back[1].wait_recv()

            @pl.when(step == 3)
            def _():
                back[2].wait_recv()
                back[3].wait_recv()

        for n in range(2):
            for d in range(2):
                for u in range(2):
                    for v in range(2):
                        at = 128 * n + 64 * d + 32 * u + 16 * v
                        xs[at : at + 16] = sc[d, 2 * band + u, 2 * n + v]
        x = xs[...]
        packed_qkv(x, cqkv, scale_s[1, 0:1])
        for n in range(2):
            attend(128 * n, 128, ones4[1], None)
        joined = x.astype(F32) + norm_rows(dot(att_s[...], cp[...]))
        contrast = jnp.concatenate(
            [joined[64:128] - joined[0:64], joined[192:256] - joined[128:192]], 0
        )
        operand = contrast.astype(BF)
        for n in range(4):
            h = dot(operand, du[:, 256 * n : 256 * n + 256])
            hid_s[0:128, 256 * n : 256 * n + 256] = gelu_twice(h).astype(BF)
        change = (contrast + norm_rows(0.5 * dot(hid_s[0:128, 0:1024], dd[...]))).astype(BF)
        oo = iota((128, 128), 0)
        tt = iota((128, 128), 1)
        r, c = oo // 16, oo % 16
        spot = (c // 8) * 64 + (r // 4) * 32 + ((c // 4) % 2) * 16 + (r % 4) * 4 + c % 4
        order = jnp.where(spot == tt, 1.0, 0.0).astype(BF)
        ob[band] = dot(order, change).astype(BF).reshape(8, 16, C)
        pltpu.make_async_copy(ob.at[band], out.at[pl.ds(8 * band, 8)], out_sem.at[band]).start()
        return carry

    lax.fori_loop(0, 4, cross_step, 0)
    for n in range(4):
        pltpu.make_async_copy(ob.at[n], out.at[pl.ds(8 * n, 8)], out_sem.at[n]).wait()
    if remote:
        for copy in halo + back:
            copy.wait_send()


def device_program(rows, cols, remote, images, labels, qkv_weight, proj_weight, up_weight, down_weight,
                   head_scale, cross_qkv, cross_proj, cross_scale, diff_up, diff_down):
    any_spec = pl.BlockSpec(memory_space=pl.ANY)
    vmem = pl.BlockSpec(memory_space=pltpu.VMEM)
    smem = pl.BlockSpec(memory_space=pltpu.SMEM)
    big = [qkv_weight, proj_weight, up_weight, down_weight, cross_qkv, cross_proj, diff_up, diff_down]
    dma = pltpu.SemaphoreType.DMA
    return pl.pallas_call(
        functools.partial(kernel, rows, cols, remote),
        out_shape=jax.ShapeDtypeStruct((32, 16, C), BF),
        in_specs=[any_spec, vmem, smem, smem] + [any_spec] * 8,
        out_specs=any_spec,
        scratch_shapes=[
            pltpu.VMEM((2, 32, 16, C), BF),
            *[pltpu.VMEM(w.shape, BF) for w in big],
            pltpu.VMEM((2, 9, 5, CELL, C), BF),
            pltpu.VMEM((9, 5, CELL, 128), BF),
            pltpu.VMEM((2, 9, 5, CELL, C), BF),
            pltpu.VMEM((256, 256), BF),
            pltpu.VMEM((256, 256), BF),
            pltpu.VMEM((2, 512, 128), BF),
            pltpu.VMEM((2, 8, C), F32),
            pltpu.VMEM((256, C), BF),
            pltpu.VMEM((256, 3 * C), BF),
            pltpu.VMEM((256, C), BF),
            pltpu.VMEM((256, 2048), BF),
            pltpu.VMEM((256, C), BF),
            pltpu.VMEM((4, 8, 16, C), BF),
            dma, dma((8,)), dma((4,)), dma((6,)), dma((6,)), dma((4,)), dma((4,)),
        ],
        compiler_params=pltpu.CompilerParams(
            collective_id=0 if remote else None,
            has_side_effects=remote,
            vmem_limit_bytes=56 * 1024 * 1024,
        ),
        cost_estimate=pl.CostEstimate(flops=11_000_000_000, bytes_accessed=13_000_000, transcendentals=6_000_000),
        name="window_pair",
    )(images, labels, head_scale, cross_scale, *big)


def solution(mesh):
    placed = (P(None, "row", "col", None), P("row", "col")) + (P(),) * 10
    body = functools.partial(device_program, mesh.shape["row"], mesh.shape["col"], True)
    return jax.shard_map(
        body, mesh=mesh, in_specs=placed, out_specs=P("row", "col", None), check_vma=False
    )
```

```python
import functools
import math

import jax
import jax.numpy as jnp
from jax import lax
from jax.experimental import pallas as pl
from jax.experimental.pallas import tpu as pltpu
from jax.sharding import PartitionSpec as P

WIN = 8
SHIFT = 4
HEADS = 16
C = 512
CELL = SHIFT * SHIFT
EPS = 1e-5
LOG2E = math.log2(math.e)
BF = jnp.bfloat16
F32 = jnp.float32
MESH = pl.DeviceIdType.MESH


def dot(a, b):
    return jnp.dot(a, b, preferred_element_type=F32)


def dot_t(a, b):
    return lax.dot_general(a, b, (((1,), (1,)), ((), ())), preferred_element_type=F32)


def iota(shape, dim):
    return lax.broadcasted_iota(jnp.int32, shape, dim)


def norm_rows(v):
    mean = jnp.sum(v, axis=-1, keepdims=True) * (1.0 / C)
    centre = v - mean
    spread = jnp.sum(centre * centre, axis=-1, keepdims=True) * (1.0 / C)
    return centre * lax.rsqrt(spread + EPS)


def pieces(count, step=64):
    return [slice(at, min(at + step, count)) for at in range(0, count, step)]


def gelu_twice(v):
    k = math.sqrt(2.0 / math.pi)
    inner = v * (k + (k * 0.044715) * (v * v))
    return v * (1.0 + jnp.tanh(inner))


NEAR = [(0, 0), (1, 0), (2, 0)]
FAR = [(0, 1), (1, 1), (2, 1), (3, 0), (3, 1)]
CROSS_NEAR = [(1, 1), (2, 1), (3, 1)]
CROSS_FAR = [(1, 0), (2, 0), (3, 0), (0, 0), (0, 1)]


def kernel(
    rows, cols, remote,
    img, lab_h, hs, cs, wqkv_h, wp_h, wu_h, wd_h, cqkv_h, cp_h, du_h, dd_h,
    out,
    im, lab, wqkv, wp, wu, wd, cqkv, cp, du, dd,
    xc, gc, sc, perm, bd, ones4, scale_s, qkv_s, att_s, hid_s, first_s, ct_s, ob,
    im_sem, lab_sem, w_sem, out_sem, send1, recv1, send2, recv2,
):
    me_r = lax.axis_index("row") if remote else 0
    me_c = lax.axis_index("col") if remote else 0
    up, down = lax.rem(me_r + rows - 1, rows), lax.rem(me_r + 1, rows)
    left, right = lax.rem(me_c + cols - 1, cols), lax.rem(me_c + 1, cols)

    weights = [
        (wqkv_h, wqkv), (wp_h, wp), (wu_h, wu), (wd_h, wd),
        (cqkv_h, cqkv), (cp_h, cp), (du_h, du), (dd_h, dd),
    ]
    loads = [pltpu.make_async_copy(s, d, w_sem.at[n]) for n, (s, d) in enumerate(weights)]
    load_im = pltpu.make_async_copy(img, im, im_sem)
    load_im.start()
    load_lab = pltpu.make_async_copy(lab_h, lab, lab_sem)
    load_lab.start()
    for load in loads:
        load.start()

    if remote:
        barrier = pltpu.get_barrier_semaphore()
        for r, c in ((up, me_c), (down, me_c), (me_r, left), (me_r, right), (up, left), (down, right)):
            pl.semaphore_signal(barrier, inc=1, device_id={"row": r, "col": c}, device_id_type=MESH)

    o = iota((256, 256), 0)
    t = iota((256, 256), 1)
    src = ((o // 64) * 4 + (o // 4) % 4) * 16 + ((o // 16) % 4) * 4 + o % 4
    perm[...] = jnp.where(src == t, 1.0, 0.0).astype(BF)

    load_im.wait()
    for d in range(2):
        for b in range(2):
            block = im[d, 16 * b : 16 * b + 16].reshape(256, C)
            cells = dot(perm[...], block).astype(BF)
            xc[d, 4 * b : 4 * b + 4, 0:4] = cells.reshape(4, 4, CELL, C)

    def send(src, dst, n, r, c, sems, rsems):
        return pltpu.make_async_remote_copy(
            src_ref=src, dst_ref=dst, send_sem=sems.at[n], recv_sem=rsems.at[n],
            device_id={"row": r, "col": c}, device_id_type=MESH,
        )

    if remote:
        pl.semaphore_wait(barrier, 6)
        halo = [
            send(xc.at[:, 1:8, 0], xc.at[:, 1:8, 4], 0, me_r, left, send1, recv1),
            send(xc.at[:, 0, 1:4], xc.at[:, 8, 1:4], 1, up, me_c, send1, recv1),
            send(xc.at[:, 0, 0], xc.at[:, 8, 4], 2, up, left, send1, recv1),
        ]
        for copy in halo:
            copy.start()

    bd[...] = jnp.where(o // 32 == t // 32, 1.0, 0.0).astype(BF)
    o4 = iota((512, 128), 0)
    t4 = iota((512, 128), 1)
    ones4[0] = jnp.where((o4 % 256) // 64 == t4 // 32, 1.0, 0.0).astype(BF)
    ones4[1] = jnp.where(o4 // 128 == t4 // 32, 1.0, 0.0).astype(BF)
    lane = iota((8, C), 1) // 32
    for n, ref in ((0, hs), (1, cs)):
        row = jnp.zeros((8, C), F32)
        for h in range(HEADS):
            row = jnp.where(lane == h, ref[h] * LOG2E, row)
        scale_s[n] = row

    load_lab.wait()
    tok = iota((512, 16), 0)
    tc = ((tok // 16) % 4) * 4 + tok % 4
    pick_c = jnp.where(tc == iota((512, 16), 1), 1.0, 0.0).astype(BF)
    tok = iota((512, 32), 0)
    tr = (tok // 64) * 4 + (tok // 4) % 4
    by_col = dot(pick_c, lab[...].astype(F32).astype(BF))
    picked = jnp.where(tr == iota((512, 32), 1), by_col, 0.0).astype(BF)
    value = dot(picked, jnp.ones((32, 128), BF)).astype(jnp.int32)
    tok = iota((512, 128), 0)
    gr = (tok // 64) * 4 + (tok // 4) % 4 + me_r * 32
    gcol = ((tok // 16) % 4) * 4 + tok % 4 + me_c * 16
    code = value * 4 + jnp.where(gr < SHIFT, 2, 0) + jnp.where(gcol < SHIFT, 1, 0)
    onehot = jnp.where(code == iota((512, 128), 1), 1.0, 0.0).astype(BF)
    gc[0:8, 0:4] = onehot.reshape(8, 4, CELL, 128)
    if remote:
        codes = [
            send(gc.at[1:8, 0], gc.at[1:8, 4], 3, me_r, left, send1, recv1),
            send(gc.at[0, 1:4], gc.at[8, 1:4], 4, up, me_c, send1, recv1),
            send(gc.at[0, 0], gc.at[8, 4], 5, up, left, send1, recv1),
        ]
        for copy in codes:
            copy.start()
        halo = halo + codes
        back = [
            send(sc.at[:, 1:8, 4], sc.at[:, 1:8, 0], 0, me_r, right, send2, recv2),
            send(sc.at[:, 8, 1:4], sc.at[:, 0, 1:4], 1, down, me_c, send2, recv2),
            send(sc.at[:, 8, 4], sc.at[:, 0, 0], 2, down, right, send2, recv2),
        ]

    head_of = iota((1, 128), 1) // 32
    head_mask = [jnp.where(head_of == h, 1.0, 0.0).astype(BF) for h in range(4)]

    def stacked(v):
        return jnp.concatenate([v * head_mask[h] for h in range(4)], 0)

    def packed_qkv(chains, w, scale):
        for n in range(6):
            lanes = slice(256 * n, 256 * n + 256)
            for base, count, x in chains:
                qkv_s[base : base + count, lanes] = dot(x(), w[:, lanes]).astype(BF)
        for n in range(4):
            lanes = slice(256 * n, 256 * n + 256)
            for base, count, x in chains:
                y = qkv_s[base : base + count, lanes]
                factor = lax.rsqrt(jnp.maximum(dot(y * y, bd[...]), 1.0))
                if n < 2:
                    factor = factor * scale[:, lanes]
                qkv_s[base : base + count, lanes] = (y.astype(F32) * factor).astype(BF)

    def attend(base, count, g, ones, mask):
        lanes = slice(128 * g, 128 * g + 128)
        q = qkv_s[base : base + count, lanes]
        k = qkv_s[base : base + count, 512 + 128 * g : 640 + 128 * g]
        v = qkv_s[base : base + count, 1024 + 128 * g : 1152 + 128 * g]
        e = jnp.exp2(dot_t(q, stacked(k))).astype(BF)
        if mask is not None:
            e = e * mask
        o = dot(e, jnp.concatenate([stacked(v), ones], 1))
        att_s[base : base + count, lanes] = (o[:, :128] * pltpu.reciprocal(o[:, 128:], approx=True)).astype(BF)

    def cells_of(ref, d, spots):
        return jnp.concatenate(
            [ref[d, i + u, j + v] for i, j in spots for u in range(2) for v in range(2)], 0
        )

    def block(windows, waits):
        spots = [(2 * a + 1, 2 * b + 1) for a, b in windows]
        count = 64 * len(spots)
        chains = [(d * count, count, functools.partial(cells_of, xc, d, spots)) for d in range(2)]
        if waits:
            loads[0].wait()
        packed_qkv(chains, wqkv, scale_s[0, 0:1])
        masks = []
        for i, j in spots:
            g = jnp.concatenate([gc[i + u, j + v] for u in range(2) for v in range(2)], 0)
            masks.append(dot_t(g, jnp.concatenate([g] * 4, 0)).astype(BF))
        for n in range(len(spots)):
            for g in range(4):
                for d in range(2):
                    attend(d * count + 64 * n, 64, g, ones4[0, 0:256], masks[n])
        if waits:
            loads[1].wait()
        for base, count, x in chains:
            v = dot(att_s[base : base + count], wp[...])
            res = x()
            for p in pieces(count):
                first = res[p].astype(F32) + norm_rows(v[p])
                first_s[base + p.start : base + p.stop] = first.astype(BF)
        if waits:
            loads[2].wait()
        for n in range(8):
            lanes = slice(256 * n, 256 * n + 256)
            for base, count, x in chains:
                h = dot(first_s[base : base + count], wu[:, lanes])
                hid_s[base : base + count, lanes] = gelu_twice(h).astype(BF)
        if waits:
            loads[3].wait()
        for d, (base, count, x) in enumerate(chains):
            v = dot(hid_s[base : base + count], wd[...])
            for n, (i, j) in enumerate(spots):
                p = slice(64 * n, 64 * n + 64)
                first = first_s[base + p.start : base + p.stop]
                second = (first.astype(F32) + norm_rows(0.5 * v[p])).astype(BF)
                for u in range(2):
                    for v2 in range(2):
                        at = 32 * u + 16 * v2
                        sc[d, i + u, j + v2] = second[at : at + 16]

    def cross(windows):
        chains = []
        for n, (a, b) in enumerate(windows):
            def x(a=a, b=b):
                return jnp.concatenate([cells_of(sc, d, [(2 * a, 2 * b)]) for d in range(2)], 0)
            chains.append((128 * n, 128, x))
        packed_qkv(chains, cqkv, scale_s[1, 0:1])
        for base, count, x in chains:
            for g in range(4):
                attend(base, count, g, ones4[1], None)
        for (base, count, x), (a, b) in zip(chains, windows):
            v = dot(att_s[base : base + count], cp[...])
            res = x()
            past = res[0:64].astype(F32) + norm_rows(v[0:64])
            ct_s[a, 64 * b : 64 * b + 64] = res[64:128].astype(F32) + norm_rows(v[64:128]) - past

    block(NEAR, True)
    if remote:
        for copy in halo:
            copy.wait_recv()
    block(FAR, False)
    if remote:
        for copy in back:
            copy.start()
    for n in range(4, 6):
        loads[n].wait()
    cross(CROSS_NEAR)
    if remote:
        for copy in back:
            copy.wait_recv()
    cross(CROSS_FAR)
    for n in range(6, 8):
        loads[n].wait()

    oo = iota((128, 128), 0)
    tt = iota((128, 128), 1)
    r, c = oo // 16, oo % 16
    spot = (c // 8) * 64 + (r // 4) * 32 + ((c // 4) % 2) * 16 + (r % 4) * 4 + c % 4
    order = jnp.where(spot == tt, 1.0, 0.0).astype(BF)
    halves = (0, 2)
    for n in range(4):
        lanes = slice(256 * n, 256 * n + 256)
        for b in halves:
            operand = ct_s[b : b + 2].reshape(256, C).astype(BF)
            hid_s[128 * b : 128 * b + 256, lanes] = gelu_twice(dot(operand, du[:, lanes])).astype(BF)
    stores = []
    for b in halves:
        v = dot(hid_s[128 * b : 128 * b + 256, 0:1024], dd[...])
        for n in range(2):
            change = jnp.concatenate(
                [
                    (ct_s[b + n, p] + norm_rows(0.5 * v[128 * n + p.start : 128 * n + p.stop])).astype(BF)
                    for p in pieces(128)
                ], 0,
            )
            ob[8 * (b + n) : 8 * (b + n) + 8] = dot(order, change).astype(BF).reshape(8, 16, C)
        store = pltpu.make_async_copy(
            ob.at[pl.ds(8 * b, 16)], out.at[pl.ds(8 * b, 16)], out_sem.at[b // 2]
        )
        store.start()
        stores.append(store)
    for store in stores:
        store.wait()
    if remote:
        for copy in halo + back:
            copy.wait_send()


def device_program(rows, cols, remote, images, labels, qkv_weight, proj_weight, up_weight, down_weight,
                   head_scale, cross_qkv, cross_proj, cross_scale, diff_up, diff_down):
    any_spec = pl.BlockSpec(memory_space=pl.ANY)
    smem = pl.BlockSpec(memory_space=pltpu.SMEM)
    big = [qkv_weight, proj_weight, up_weight, down_weight, cross_qkv, cross_proj, diff_up, diff_down]
    dma = pltpu.SemaphoreType.DMA
    return pl.pallas_call(
        functools.partial(kernel, rows, cols, remote),
        out_shape=jax.ShapeDtypeStruct((32, 16, C), BF),
        in_specs=[any_spec, any_spec, smem, smem] + [any_spec] * 8,
        out_specs=any_spec,
        scratch_shapes=[
            pltpu.VMEM((2, 32, 16, C), BF),
            pltpu.VMEM((16, 32), jnp.int32),
            *[pltpu.VMEM(w.shape, BF) for w in big],
            pltpu.VMEM((2, 9, 5, CELL, C), BF),
            pltpu.VMEM((9, 5, CELL, 128), BF),
            pltpu.VMEM((2, 9, 5, CELL, C), BF),
            pltpu.VMEM((256, 256), BF),
            pltpu.VMEM((256, 256), BF),
            pltpu.VMEM((2, 512, 128), BF),
            pltpu.VMEM((2, 8, C), F32),
            pltpu.VMEM((640, 3 * C), BF),
            pltpu.VMEM((640, C), BF),
            pltpu.VMEM((640, 2048), BF),
            pltpu.VMEM((640, C), BF),
            pltpu.VMEM((4, 128, C), F32),
            pltpu.VMEM((32, 16, C), BF),
            dma, dma, dma((8,)), dma((2,)), dma((6,)), dma((6,)), dma((3,)), dma((3,)),
        ],
        compiler_params=pltpu.CompilerParams(
            collective_id=0 if remote else None,
            has_side_effects=remote,
            vmem_limit_bytes=56 * 1024 * 1024,
        ),
        cost_estimate=pl.CostEstimate(flops=11_000_000_000, bytes_accessed=13_000_000, transcendentals=6_000_000),
        name="window_pair",
    )(images, labels.T, head_scale, cross_scale, *big)


def solution(mesh):
    placed = (P(None, "row", "col", None), P("row", "col")) + (P(),) * 10
    body = functools.partial(device_program, mesh.shape["row"], mesh.shape["col"], True)
    return jax.shard_map(
        body, mesh=mesh, in_specs=placed, out_specs=P("row", "col", None), check_vma=False
    )
```

```python
import functools
import math

import jax
import jax.numpy as jnp
from jax import lax
from jax.experimental import pallas as pl
from jax.experimental.pallas import tpu as pltpu
from jax.sharding import PartitionSpec as P

WIN = 8
SHIFT = 4
HEADS = 16
C = 512
CELL = SHIFT * SHIFT
EPS = 1e-5
LOG2E = math.log2(math.e)
BF = jnp.bfloat16
F32 = jnp.float32
MESH = pl.DeviceIdType.MESH


def dot(a, b):
    return jnp.dot(a, b, preferred_element_type=F32)


def dot_t(a, b):
    return lax.dot_general(a, b, (((1,), (1,)), ((), ())), preferred_element_type=F32)


def iota(shape, dim):
    return lax.broadcasted_iota(jnp.int32, shape, dim)


def norm_rows(v):
    mean = jnp.sum(v, axis=-1, keepdims=True) * (1.0 / C)
    centre = v - mean
    spread = jnp.sum(centre * centre, axis=-1, keepdims=True) * (1.0 / C)
    return centre * lax.rsqrt(spread + EPS)


def pieces(count, step=64):
    return [slice(at, min(at + step, count)) for at in range(0, count, step)]


def gelu_twice(v):
    k = math.sqrt(2.0 / math.pi)
    inner = v * (k + (k * 0.044715) * (v * v))
    return v * (1.0 + jnp.tanh(inner))


BLOCK = [(d, a, 0) for d in range(2) for a in range(3)]
BLOCK += [(d, a, b) for d in range(2) for a, b in ((0, 1), (1, 1), (2, 1), (3, 0), (3, 1))]
BLOCK_NEAR, BLOCK_FAR = (0, 3, 6), (6, 11, 16)
CROSS = [(1, 1), (2, 1), (3, 1), (1, 0), (2, 0), (3, 0), (0, 0), (0, 1)]
CROSS_NEAR, CROSS_FAR = range(3), range(3, 8)


def cell_rows():
    block, cross = [], []
    for n, (d, a, b) in enumerate(BLOCK):
        for u in range(2):
            for v in range(2):
                block.append(((d, 2 * a + 1 + u, 2 * b + 1 + v), 64 * n + 32 * u + 16 * v))
    for n, (a, b) in enumerate(CROSS):
        for d in range(2):
            for u in range(2):
                for v in range(2):
                    cross.append(((d, 2 * a + u, 2 * b + v), 128 * n + 64 * d + 32 * u + 16 * v))
    return block, cross


def kernel(
    rows, cols, remote,
    img, lab_h, hs, cs, wqkv_h, wp_h, wu_h, wd_h, cqkv_h, cp_h, du_h, dd_h,
    out,
    im, lab, wqkv, wp, wu, wd, cqkv, cp, du, dd,
    xc, gc, sc, perm, bd, ones4, scale_s, qkv_s, att_s, hid_s, first_s, ct_s, ob,
    im_sem, lab_sem, w_sem, out_sem, send1, recv1, send2, recv2,
):
    me_r = lax.axis_index("row") if remote else 0
    me_c = lax.axis_index("col") if remote else 0
    up, down = lax.rem(me_r + rows - 1, rows), lax.rem(me_r + 1, rows)
    left, right = lax.rem(me_c + cols - 1, cols), lax.rem(me_c + 1, cols)

    weights = [
        (wqkv_h, wqkv), (wp_h, wp), (wu_h, wu), (wd_h, wd),
        (cqkv_h, cqkv), (cp_h, cp), (du_h, du), (dd_h, dd),
    ]
    loads = [pltpu.make_async_copy(s, d, w_sem.at[n]) for n, (s, d) in enumerate(weights)]
    load_im = pltpu.make_async_copy(img, im, im_sem)
    load_im.start()
    load_lab = pltpu.make_async_copy(lab_h, lab, lab_sem)
    load_lab.start()
    loads[0].start()

    if remote:
        barrier = pltpu.get_barrier_semaphore()
        for r, c in ((up, me_c), (down, me_c), (me_r, left), (me_r, right), (up, left), (down, right)):
            pl.semaphore_signal(barrier, inc=1, device_id={"row": r, "col": c}, device_id_type=MESH)

    o = iota((256, 256), 0)
    t = iota((256, 256), 1)
    src = (((o >> 6) * 4 + ((o >> 2) & 3)) * 16) + ((o >> 4) & 3) * 4 + (o & 3)
    perm[...] = jnp.where(src == t, 1.0, 0.0).astype(BF)

    load_im.wait()
    for load in loads[1:4]:
        load.start()
    for d in range(2):
        for b in range(2):
            block = im[d, 16 * b : 16 * b + 16].reshape(256, C)
            cells = dot(perm[...], block).astype(BF)
            xc[d, 4 * b : 4 * b + 4, 0:4] = cells.reshape(4, 4, CELL, C)

    def send(src, dst, n, r, c, sems, rsems):
        return pltpu.make_async_remote_copy(
            src_ref=src, dst_ref=dst, send_sem=sems.at[n], recv_sem=rsems.at[n],
            device_id={"row": r, "col": c}, device_id_type=MESH,
        )

    block_cells, cross_cells = cell_rows()

    def project(ref, cells, w):
        for n in range(6):
            lanes = slice(256 * n, 256 * n + 256)
            for part in cells:
                y = dot(jnp.concatenate([ref[spot] for spot, _ in part], 0), w[:, lanes]).astype(BF)
                for m, (_, row) in enumerate(part):
                    qkv_s[row : row + 16, lanes] = y[16 * m : 16 * m + 16]

    def unit(cells, scale):
        for n in range(4):
            lanes = slice(256 * n, 256 * n + 256)
            for part in cells:
                y = jnp.concatenate([qkv_s[row : row + 16, lanes] for _, row in part], 0)
                factor = lax.rsqrt(jnp.maximum(dot(y * y, bd[...]), 1.0))
                if n < 2:
                    factor = factor * scale[:, lanes]
                y = (y.astype(F32) * factor).astype(BF)
                for m, (_, row) in enumerate(part):
                    qkv_s[row : row + 16, lanes] = y[16 * m : 16 * m + 16]

    def by_date(cells, here):
        return [[c for c in cells if c[0][0] == d and here(c[0]) ] for d in range(2)]

    own_block = by_date(block_cells, lambda c: c[1] < 8 and c[2] < 4)
    far_block = by_date(block_cells, lambda c: not (c[1] < 8 and c[2] < 4))
    own_cross = by_date(cross_cells, lambda c: c[1] > 0 and c[2] > 0)
    far_cross = by_date(cross_cells, lambda c: not (c[1] > 0 and c[2] > 0))

    loads[0].wait()
    project(xc, own_block, wqkv)
    for load in loads[4:]:
        load.start()

    if remote:
        pl.semaphore_wait(barrier, 6)
        halo = [
            send(xc.at[:, 1:8, 0], xc.at[:, 1:8, 4], 0, me_r, left, send1, recv1),
            send(xc.at[:, 0, 1:4], xc.at[:, 8, 1:4], 1, up, me_c, send1, recv1),
            send(xc.at[:, 0, 0], xc.at[:, 8, 4], 2, up, left, send1, recv1),
        ]
        for copy in halo:
            copy.start()

    bd[...] = jnp.where((o >> 5) == (t >> 5), 1.0, 0.0).astype(BF)
    o4 = iota((512, 128), 0)
    t4 = iota((512, 128), 1)
    ones4[0] = jnp.where(((o4 >> 6) & 3) == (t4 >> 5), 1.0, 0.0).astype(BF)
    ones4[1] = jnp.where((o4 >> 7) == (t4 >> 5), 1.0, 0.0).astype(BF)
    lane = iota((8, C), 1) >> 5
    for n, ref in ((0, hs), (1, cs)):
        row = jnp.zeros((8, C), F32)
        for h in range(HEADS):
            row = jnp.where(lane == h, ref[h] * LOG2E, row)
        scale_s[n] = row

    unit(own_block, scale_s[0, 0:1])

    load_lab.wait()
    tok = iota((512, 16), 0)
    tc = ((tok >> 4) & 3) * 4 + (tok & 3)
    pick_c = jnp.where(tc == iota((512, 16), 1), 1.0, 0.0).astype(BF)
    tok = iota((512, 32), 0)
    tr = (tok >> 6) * 4 + ((tok >> 2) & 3)
    by_col = dot(pick_c, lab[...].astype(F32).astype(BF))
    picked = jnp.where(tr == iota((512, 32), 1), by_col, 0.0).astype(BF)
    value = dot(picked, jnp.ones((32, 128), BF)).astype(jnp.int32)
    tok = iota((512, 128), 0)
    gr = (tok >> 6) * 4 + ((tok >> 2) & 3) + me_r * 32
    gcol = ((tok >> 4) & 3) * 4 + (tok & 3) + me_c * 16
    code = value * 4 + jnp.where(gr < SHIFT, 2, 0) + jnp.where(gcol < SHIFT, 1, 0)
    onehot = jnp.where(code == iota((512, 128), 1), 1.0, 0.0).astype(BF)
    gc[0:8, 0:4] = onehot.reshape(8, 4, CELL, 128)
    if remote:
        codes = [
            send(gc.at[1:8, 0], gc.at[1:8, 4], 3, me_r, left, send1, recv1),
            send(gc.at[0, 1:4], gc.at[8, 1:4], 4, up, me_c, send1, recv1),
            send(gc.at[0, 0], gc.at[8, 4], 5, up, left, send1, recv1),
        ]
        for copy in codes:
            copy.start()
        halo = halo + codes
        back = [
            send(sc.at[:, 1:8, 4], sc.at[:, 1:8, 0], 0, me_r, right, send2, recv2),
            send(sc.at[:, 8, 1:4], sc.at[:, 0, 1:4], 1, down, me_c, send2, recv2),
            send(sc.at[:, 8, 4], sc.at[:, 0, 0], 2, down, right, send2, recv2),
        ]

    head_of = iota((1, 128), 1) >> 5
    head_mask = [jnp.where(head_of == h, 1.0, 0.0).astype(BF) for h in range(4)]

    def stacked(v):
        return jnp.concatenate([v * head_mask[h] for h in range(4)], 0)

    def attend(base, count, g, ones, mask):
        lanes = slice(128 * g, 128 * g + 128)
        q = qkv_s[base : base + count, lanes]
        k = qkv_s[base : base + count, 512 + 128 * g : 640 + 128 * g]
        v = qkv_s[base : base + count, 1024 + 128 * g : 1152 + 128 * g]
        e = jnp.exp2(dot_t(q, stacked(k))).astype(BF)
        if mask is not None:
            e = e * mask
        o = dot(e, jnp.concatenate([stacked(v), ones], 1))
        att_s[base : base + count, lanes] = (o[:, :128] * pltpu.reciprocal(o[:, 128:], approx=True)).astype(BF)

    def cells_of(ref, d, i, j):
        return [ref[d, i + u, j + v] for u in range(2) for v in range(2)]

    def spot_of(n):
        d, a, b = BLOCK[n]
        return d, 2 * a + 1, 2 * b + 1

    def block(first_n, mid_n, last_n, waits):
        chains = [(64 * lo, 64 * hi) for lo, hi in ((first_n, mid_n), (mid_n, last_n))]
        for n in range(first_n, mid_n):
            _, i, j = spot_of(n)
            g = jnp.concatenate([gc[i + u, j + v] for u in range(2) for v in range(2)], 0)
            mask = dot_t(g, jnp.concatenate([g] * 4, 0)).astype(BF)
            for g in range(4):
                for m in (n, n + mid_n - first_n):
                    attend(64 * m, 64, g, ones4[0, 0:256], mask)
        if waits:
            loads[1].wait()
        for lo, hi in chains:
            v = dot(att_s[lo:hi], wp[...])
            for row in range(lo, hi, 64):
                res = jnp.concatenate(cells_of(xc, *spot_of(row // 64)), 0)
                first = res.astype(F32) + norm_rows(v[row - lo : row - lo + 64])
                first_s[row : row + 64] = first.astype(BF)
        if waits:
            loads[2].wait()
        for n in range(8):
            lanes = slice(256 * n, 256 * n + 256)
            for lo, hi in chains:
                hid_s[lo:hi, lanes] = gelu_twice(dot(first_s[lo:hi], wu[:, lanes])).astype(BF)
        if waits:
            loads[3].wait()
        for lo, hi in chains:
            v = dot(hid_s[lo:hi], wd[...])
            for row in range(lo, hi, 64):
                d, i, j = spot_of(row // 64)
                first = first_s[row : row + 64].astype(F32)
                second = (first + norm_rows(0.5 * v[row - lo : row - lo + 64])).astype(BF)
                for u in range(2):
                    for v2 in range(2):
                        at = 32 * u + 16 * v2
                        sc[d, i + u, j + v2] = second[at : at + 16]

    def cross(windows):
        for n in windows:
            for g in range(4):
                attend(128 * n, 128, g, ones4[1], None)
        for n in windows:
            a, b = CROSS[n]
            v = dot(att_s[128 * n : 128 * n + 128], cp[...])
            res = [jnp.concatenate(cells_of(sc, d, 2 * a, 2 * b), 0).astype(F32) for d in range(2)]
            past = res[0] + norm_rows(v[0:64])
            ct_s[a, 64 * b : 64 * b + 64] = res[1] + norm_rows(v[64:128]) - past

    block(*BLOCK_NEAR, True)
    if remote:
        for copy in halo:
            copy.wait_recv()
    project(xc, far_block, wqkv)
    unit(far_block, scale_s[0, 0:1])
    block(*BLOCK_FAR, False)
    if remote:
        for copy in back:
            copy.start()
    for n in range(4, 6):
        loads[n].wait()
    project(sc, own_cross, cqkv)
    unit(own_cross, scale_s[1, 0:1])
    cross(CROSS_NEAR)
    if remote:
        for copy in back:
            copy.wait_recv()
    project(sc, far_cross, cqkv)
    unit(far_cross, scale_s[1, 0:1])
    cross(CROSS_FAR)
    for n in range(6, 8):
        loads[n].wait()

    oo = iota((128, 128), 0)
    tt = iota((128, 128), 1)
    r, c = oo >> 4, oo & 15
    spot = (c >> 3) * 64 + (r >> 2) * 32 + ((c >> 2) & 1) * 16 + (r & 3) * 4 + (c & 3)
    order = jnp.where(spot == tt, 1.0, 0.0).astype(BF)
    halves = (0, 2)
    for n in range(4):
        lanes = slice(256 * n, 256 * n + 256)
        for b in halves:
            operand = ct_s[b : b + 2].reshape(256, C).astype(BF)
            hid_s[128 * b : 128 * b + 256, lanes] = gelu_twice(dot(operand, du[:, lanes])).astype(BF)
    for b in halves:
        v = dot(hid_s[128 * b : 128 * b + 256, 0:1024], dd[...])
        for n in range(2):
            change = jnp.concatenate(
                [
                    (ct_s[b + n, p] + norm_rows(0.5 * v[128 * n + p.start : 128 * n + p.stop])).astype(BF)
                    for p in pieces(128)
                ], 0,
            )
            out[8 * (b + n) : 8 * (b + n) + 8] = dot(order, change).astype(BF).reshape(8, 16, C)
    if remote:
        for copy in halo + back:
            copy.wait_send()


def device_program(rows, cols, remote, images, labels, qkv_weight, proj_weight, up_weight, down_weight,
                   head_scale, cross_qkv, cross_proj, cross_scale, diff_up, diff_down):
    any_spec = pl.BlockSpec(memory_space=pl.ANY)
    smem = pl.BlockSpec(memory_space=pltpu.SMEM)
    big = [qkv_weight, proj_weight, up_weight, down_weight, cross_qkv, cross_proj, diff_up, diff_down]
    dma = pltpu.SemaphoreType.DMA
    return pl.pallas_call(
        functools.partial(kernel, rows, cols, remote),
        out_shape=pltpu.VMEM((32, 16, C), BF),
        in_specs=[any_spec, any_spec, smem, smem] + [any_spec] * 8,
        out_specs=pl.BlockSpec(memory_space=pltpu.VMEM),
        scratch_shapes=[
            pltpu.VMEM((2, 32, 16, C), BF),
            pltpu.VMEM((16, 32), jnp.int32),
            *[pltpu.VMEM(w.shape, BF) for w in big],
            pltpu.VMEM((2, 9, 5, CELL, C), BF),
            pltpu.VMEM((9, 5, CELL, 128), BF),
            pltpu.VMEM((2, 9, 5, CELL, C), BF),
            pltpu.VMEM((256, 256), BF),
            pltpu.VMEM((256, 256), BF),
            pltpu.VMEM((2, 512, 128), BF),
            pltpu.VMEM((2, 8, C), F32),
            pltpu.VMEM((1024, 3 * C), BF),
            pltpu.VMEM((1024, C), BF),
            pltpu.VMEM((1024, 2048), BF),
            pltpu.VMEM((1024, C), BF),
            pltpu.VMEM((4, 128, C), F32),
            pltpu.VMEM((32, 16, C), BF),
            dma, dma, dma((8,)), dma((2,)), dma((6,)), dma((6,)), dma((3,)), dma((3,)),
        ],
        compiler_params=pltpu.CompilerParams(
            collective_id=0 if remote else None,
            has_side_effects=remote,
            vmem_limit_bytes=60 * 1024 * 1024,
        ),
        cost_estimate=pl.CostEstimate(flops=11_000_000_000, bytes_accessed=13_000_000, transcendentals=6_000_000),
        name="window_pair",
    )(images, labels.T, head_scale, cross_scale, *big)


def solution(mesh):
    placed = (P(None, "row", "col", None), P("row", "col")) + (P(),) * 10
    body = functools.partial(device_program, mesh.shape["row"], mesh.shape["col"], True)
    return jax.shard_map(
        body, mesh=mesh, in_specs=placed, out_specs=P("row", "col", None), check_vma=False
    )
```

```python
import functools
import math

import jax
import jax.numpy as jnp
from jax import lax
from jax.experimental import pallas as pl
from jax.experimental.pallas import tpu as pltpu
from jax.sharding import PartitionSpec as P

WIN = 8
SHIFT = 4
HEADS = 16
C = 512
CELL = SHIFT * SHIFT
EPS = 1e-5
LOG2E = math.log2(math.e)
BF = jnp.bfloat16
F32 = jnp.float32
MESH = pl.DeviceIdType.MESH


def dot(a, b):
    return jnp.dot(a, b, preferred_element_type=F32)


def dot_t(a, b):
    return lax.dot_general(a, b, (((1,), (1,)), ((), ())), preferred_element_type=F32)


def iota(shape, dim):
    return lax.broadcasted_iota(jnp.int32, shape, dim)


def norm_rows(v):
    mean = jnp.sum(v, axis=-1, keepdims=True) * (1.0 / C)
    centre = v - mean
    spread = jnp.sum(centre * centre, axis=-1, keepdims=True) * (1.0 / C)
    return centre * lax.rsqrt(spread + EPS)


def pieces(count, step=64):
    return [slice(at, min(at + step, count)) for at in range(0, count, step)]


def gelu_twice(v):
    k = math.sqrt(2.0 / math.pi)
    inner = v * (k + (k * 0.044715) * (v * v))
    return v * (1.0 + jnp.tanh(inner))


BLOCK = [(d, a, 0) for d in range(2) for a in range(3)]
BLOCK += [(d, a, b) for d in range(2) for a, b in ((0, 1), (1, 1), (2, 1), (3, 0), (3, 1))]
BLOCK_NEAR, BLOCK_FAR = (0, 3, 6), (6, 11, 16)
CROSS = [(1, 1), (2, 1), (3, 1), (1, 0), (2, 0), (3, 0), (0, 0), (0, 1)]
CROSS_NEAR, CROSS_FAR = range(3), range(3, 8)


def cell_rows():
    block, cross = [], []
    for n, (d, a, b) in enumerate(BLOCK):
        for u in range(2):
            for v in range(2):
                block.append(((d, 2 * a + 1 + u, 2 * b + 1 + v), 64 * n + 32 * u + 16 * v))
    for n, (a, b) in enumerate(CROSS):
        for d in range(2):
            for u in range(2):
                for v in range(2):
                    cross.append(((d, 2 * a + u, 2 * b + v), 128 * n + 64 * d + 32 * u + 16 * v))
    return block, cross


def kernel(
    rows, cols, remote,
    img, lab_h, hs, cs, wqkv_h, wp_h, wu_h, wd_h, cqkv_h, cp_h, du_h, dd_h,
    out,
    im, lab, wqkv, wp, wu, wd, cqkv, cp, du, dd,
    xc, gc, sc, perm, bd, ones4, scale_s, qkv_s, att_s, hid_s, first_s, ct_s, ob,
    im_sem, lab_sem, w_sem, out_sem, send1, recv1, send2, recv2,
):
    me_r = lax.axis_index("row") if remote else 0
    me_c = lax.axis_index("col") if remote else 0
    up, down = lax.rem(me_r + rows - 1, rows), lax.rem(me_r + 1, rows)
    left, right = lax.rem(me_c + cols - 1, cols), lax.rem(me_c + 1, cols)

    early = lax.rem(me_c, cols // 2) == 0

    weights = [
        (wqkv_h, wqkv), (wp_h, wp), (wu_h, wu), (wd_h, wd),
        (cqkv_h, cqkv), (cp_h, cp), (du_h, du), (dd_h, dd),
    ]
    loads = [pltpu.make_async_copy(s, d, w_sem.at[n]) for n, (s, d) in enumerate(weights)]
    load_im = pltpu.make_async_copy(img, im, im_sem)
    load_im.start()
    load_lab = pltpu.make_async_copy(lab_h, lab, lab_sem)
    load_lab.start()
    loads[0].start()

    if remote:
        barrier = pltpu.get_barrier_semaphore()
        for r, c in ((up, me_c), (down, me_c), (me_r, left), (me_r, right), (up, left), (down, right)):
            pl.semaphore_signal(barrier, inc=1, device_id={"row": r, "col": c}, device_id_type=MESH)

    o = iota((256, 256), 0)
    t = iota((256, 256), 1)
    src = (((o >> 6) * 4 + ((o >> 2) & 3)) * 16) + ((o >> 4) & 3) * 4 + (o & 3)
    perm[...] = jnp.where(src == t, 1.0, 0.0).astype(BF)

    load_im.wait()
    for load in loads[1:4]:
        load.start()
    for d in range(2):
        for b in range(2):
            block = im[d, 16 * b : 16 * b + 16].reshape(256, C)
            cells = dot(perm[...], block).astype(BF)
            xc[d, 4 * b : 4 * b + 4, 0:4] = cells.reshape(4, 4, CELL, C)

    def send(src, dst, n, r, c, sems, rsems):
        return pltpu.make_async_remote_copy(
            src_ref=src, dst_ref=dst, send_sem=sems.at[n], recv_sem=rsems.at[n],
            device_id={"row": r, "col": c}, device_id_type=MESH,
        )

    block_cells, cross_cells = cell_rows()

    def project(ref, cells, w):
        for n in range(6):
            lanes = slice(256 * n, 256 * n + 256)
            for part in cells:
                y = dot(jnp.concatenate([ref[spot] for spot, _ in part], 0), w[:, lanes]).astype(BF)
                for m, (_, row) in enumerate(part):
                    qkv_s[row : row + 16, lanes] = y[16 * m : 16 * m + 16]

    def unit(cells, scale):
        for n in range(4):
            lanes = slice(256 * n, 256 * n + 256)
            for part in cells:
                y = jnp.concatenate([qkv_s[row : row + 16, lanes] for _, row in part], 0)
                factor = lax.rsqrt(jnp.maximum(dot(y * y, bd[...]), 1.0))
                if n < 2:
                    factor = factor * scale[:, lanes]
                y = (y.astype(F32) * factor).astype(BF)
                for m, (_, row) in enumerate(part):
                    qkv_s[row : row + 16, lanes] = y[16 * m : 16 * m + 16]

    def by_date(cells, here):
        return [[c for c in cells if c[0][0] == d and here(c[0]) ] for d in range(2)]

    own_block = by_date(block_cells, lambda c: c[1] < 8 and c[2] < 4)
    far_block = by_date(block_cells, lambda c: not (c[1] < 8 and c[2] < 4))
    own_cross = by_date(cross_cells, lambda c: c[1] > 0 and c[2] > 0)
    far_cross = by_date(cross_cells, lambda c: not (c[1] > 0 and c[2] > 0))

    def on(condition):
        return pl.when(condition) if remote else (lambda work: work())

    if remote:
        halo = [
            send(xc.at[:, 1:8, 0], xc.at[:, 1:8, 4], 0, me_r, left, send1, recv1),
            send(xc.at[:, 0, 1:4], xc.at[:, 8, 1:4], 1, up, me_c, send1, recv1),
            send(xc.at[:, 0, 0], xc.at[:, 8, 4], 2, up, left, send1, recv1),
            send(gc.at[1:8, 0], gc.at[1:8, 4], 3, me_r, left, send1, recv1),
            send(gc.at[0, 1:4], gc.at[8, 1:4], 4, up, me_c, send1, recv1),
            send(gc.at[0, 0], gc.at[8, 4], 5, up, left, send1, recv1),
        ]

        @pl.when(jnp.logical_not(early))
        def _():
            pl.semaphore_wait(barrier, 6)
            for copy in halo[:3]:
                copy.start()

    loads[0].wait()
    project(xc, own_block, wqkv)
    for load in loads[4:]:
        load.start()

    bd[...] = jnp.where((o >> 5) == (t >> 5), 1.0, 0.0).astype(BF)
    o4 = iota((512, 128), 0)
    t4 = iota((512, 128), 1)
    ones4[0] = jnp.where(((o4 >> 6) & 3) == (t4 >> 5), 1.0, 0.0).astype(BF)
    ones4[1] = jnp.where((o4 >> 7) == (t4 >> 5), 1.0, 0.0).astype(BF)
    lane = iota((8, C), 1) >> 5
    for n, ref in ((0, hs), (1, cs)):
        row = jnp.zeros((8, C), F32)
        for h in range(HEADS):
            row = jnp.where(lane == h, ref[h] * LOG2E, row)
        scale_s[n] = row

    unit(own_block, scale_s[0, 0:1])

    load_lab.wait()
    tok = iota((512, 16), 0)
    tc = ((tok >> 4) & 3) * 4 + (tok & 3)
    pick_c = jnp.where(tc == iota((512, 16), 1), 1.0, 0.0).astype(BF)
    tok = iota((512, 32), 0)
    tr = (tok >> 6) * 4 + ((tok >> 2) & 3)
    by_col = dot(pick_c, lab[...].astype(F32).astype(BF))
    picked = jnp.where(tr == iota((512, 32), 1), by_col, 0.0).astype(BF)
    value = dot(picked, jnp.ones((32, 128), BF)).astype(jnp.int32)
    tok = iota((512, 128), 0)
    gr = (tok >> 6) * 4 + ((tok >> 2) & 3) + me_r * 32
    gcol = ((tok >> 4) & 3) * 4 + (tok & 3) + me_c * 16
    code = value * 4 + jnp.where(gr < SHIFT, 2, 0) + jnp.where(gcol < SHIFT, 1, 0)
    onehot = jnp.where(code == iota((512, 128), 1), 1.0, 0.0).astype(BF)
    gc[0:8, 0:4] = onehot.reshape(8, 4, CELL, 128)
    if remote:
        @pl.when(jnp.logical_not(early))
        def _():
            for copy in halo[3:]:
                copy.start()

        back = [
            send(sc.at[:, 1:8, 4], sc.at[:, 1:8, 0], 0, me_r, right, send2, recv2),
            send(sc.at[:, 8, 1:4], sc.at[:, 0, 1:4], 1, down, me_c, send2, recv2),
            send(sc.at[:, 8, 4], sc.at[:, 0, 0], 2, down, right, send2, recv2),
        ]

    head_of = iota((1, 128), 1) >> 5
    head_mask = [jnp.where(head_of == h, 1.0, 0.0).astype(BF) for h in range(4)]

    def stacked(v):
        return jnp.concatenate([v * head_mask[h] for h in range(4)], 0)

    def attend(base, count, g, ones, mask):
        lanes = slice(128 * g, 128 * g + 128)
        q = qkv_s[base : base + count, lanes]
        k = qkv_s[base : base + count, 512 + 128 * g : 640 + 128 * g]
        v = qkv_s[base : base + count, 1024 + 128 * g : 1152 + 128 * g]
        e = jnp.exp2(dot_t(q, stacked(k))).astype(BF)
        if mask is not None:
            e = e * mask
        o = dot(e, jnp.concatenate([stacked(v), ones], 1))
        att_s[base : base + count, lanes] = (o[:, :128] * pltpu.reciprocal(o[:, 128:], approx=True)).astype(BF)

    def cells_of(ref, d, i, j):
        return [ref[d, i + u, j + v] for u in range(2) for v in range(2)]

    def spot_of(n):
        d, a, b = BLOCK[n]
        return d, 2 * a + 1, 2 * b + 1

    def block(first_n, mid_n, last_n, waits):
        chains = [(64 * lo, 64 * hi) for lo, hi in ((first_n, mid_n), (mid_n, last_n))]
        for n in range(first_n, mid_n):
            _, i, j = spot_of(n)
            g = jnp.concatenate([gc[i + u, j + v] for u in range(2) for v in range(2)], 0)
            mask = dot_t(g, jnp.concatenate([g] * 4, 0)).astype(BF)
            for g in range(4):
                for m in (n, n + mid_n - first_n):
                    attend(64 * m, 64, g, ones4[0, 0:256], mask)
        if waits:
            loads[1].wait()
        for lo, hi in chains:
            v = dot(att_s[lo:hi], wp[...])
            for row in range(lo, hi, 64):
                res = jnp.concatenate(cells_of(xc, *spot_of(row // 64)), 0)
                first = res.astype(F32) + norm_rows(v[row - lo : row - lo + 64])
                first_s[row : row + 64] = first.astype(BF)
        if waits:
            loads[2].wait()
        for n in range(8):
            lanes = slice(256 * n, 256 * n + 256)
            for lo, hi in chains:
                hid_s[lo:hi, lanes] = gelu_twice(dot(first_s[lo:hi], wu[:, lanes])).astype(BF)
        if waits:
            loads[3].wait()
        for lo, hi in chains:
            v = dot(hid_s[lo:hi], wd[...])
            for row in range(lo, hi, 64):
                d, i, j = spot_of(row // 64)
                first = first_s[row : row + 64].astype(F32)
                second = (first + norm_rows(0.5 * v[row - lo : row - lo + 64])).astype(BF)
                for u in range(2):
                    for v2 in range(2):
                        at = 32 * u + 16 * v2
                        sc[d, i + u, j + v2] = second[at : at + 16]

    def cross(windows):
        for n in windows:
            for g in range(4):
                attend(128 * n, 128, g, ones4[1], None)
        for n in windows:
            a, b = CROSS[n]
            v = dot(att_s[128 * n : 128 * n + 128], cp[...])
            res = [jnp.concatenate(cells_of(sc, d, 2 * a, 2 * b), 0).astype(F32) for d in range(2)]
            past = res[0] + norm_rows(v[0:64])
            ct_s[a, 64 * b : 64 * b + 64] = res[1] + norm_rows(v[64:128]) - past

    if remote:
        @pl.when(early)
        def _():
            block(*BLOCK_NEAR, True)
            pl.semaphore_wait(barrier, 6)
            for copy in halo:
                copy.start()

        for copy in halo:
            copy.wait_recv()
    project(xc, far_block, wqkv)
    unit(far_block, scale_s[0, 0:1])

    @on(jnp.logical_not(early))
    def _():
        for n in range(1, 4):
            loads[n].wait()

    block(*BLOCK_FAR, False)
    if remote:
        for copy in back:
            copy.start()

    @on(jnp.logical_not(early))
    def _():
        block(*BLOCK_NEAR, False)

    for n in range(4, 6):
        loads[n].wait()
    project(sc, own_cross, cqkv)
    unit(own_cross, scale_s[1, 0:1])
    cross(CROSS_NEAR)
    if remote:
        for copy in back:
            copy.wait_recv()
    project(sc, far_cross, cqkv)
    unit(far_cross, scale_s[1, 0:1])
    cross(CROSS_FAR)
    for n in range(6, 8):
        loads[n].wait()

    oo = iota((128, 128), 0)
    tt = iota((128, 128), 1)
    r, c = oo >> 4, oo & 15
    spot = (c >> 3) * 64 + (r >> 2) * 32 + ((c >> 2) & 1) * 16 + (r & 3) * 4 + (c & 3)
    order = jnp.where(spot == tt, 1.0, 0.0).astype(BF)
    halves = (0, 2)
    for n in range(4):
        lanes = slice(256 * n, 256 * n + 256)
        for b in halves:
            operand = ct_s[b : b + 2].reshape(256, C).astype(BF)
            hid_s[128 * b : 128 * b + 256, lanes] = gelu_twice(dot(operand, du[:, lanes])).astype(BF)
    for b in halves:
        v = dot(hid_s[128 * b : 128 * b + 256, 0:1024], dd[...])
        for n in range(2):
            change = jnp.concatenate(
                [
                    (ct_s[b + n, p] + norm_rows(0.5 * v[128 * n + p.start : 128 * n + p.stop])).astype(BF)
                    for p in pieces(128)
                ], 0,
            )
            out[8 * (b + n) : 8 * (b + n) + 8] = dot(order, change).astype(BF).reshape(8, 16, C)
    if remote:
        for copy in halo + back:
            copy.wait_send()


def device_program(rows, cols, remote, images, labels, qkv_weight, proj_weight, up_weight, down_weight,
                   head_scale, cross_qkv, cross_proj, cross_scale, diff_up, diff_down):
    any_spec = pl.BlockSpec(memory_space=pl.ANY)
    smem = pl.BlockSpec(memory_space=pltpu.SMEM)
    big = [qkv_weight, proj_weight, up_weight, down_weight, cross_qkv, cross_proj, diff_up, diff_down]
    dma = pltpu.SemaphoreType.DMA
    return pl.pallas_call(
        functools.partial(kernel, rows, cols, remote),
        out_shape=pltpu.VMEM((32, 16, C), BF),
        in_specs=[any_spec, any_spec, smem, smem] + [any_spec] * 8,
        out_specs=pl.BlockSpec(memory_space=pltpu.VMEM),
        scratch_shapes=[
            pltpu.VMEM((2, 32, 16, C), BF),
            pltpu.VMEM((16, 32), jnp.int32),
            *[pltpu.VMEM(w.shape, BF) for w in big],
            pltpu.VMEM((2, 9, 5, CELL, C), BF),
            pltpu.VMEM((9, 5, CELL, 128), BF),
            pltpu.VMEM((2, 9, 5, CELL, C), BF),
            pltpu.VMEM((256, 256), BF),
            pltpu.VMEM((256, 256), BF),
            pltpu.VMEM((2, 512, 128), BF),
            pltpu.VMEM((2, 8, C), F32),
            pltpu.VMEM((1024, 3 * C), BF),
            pltpu.VMEM((1024, C), BF),
            pltpu.VMEM((1024, 2048), BF),
            pltpu.VMEM((1024, C), BF),
            pltpu.VMEM((4, 128, C), F32),
            pltpu.VMEM((32, 16, C), BF),
            dma, dma, dma((8,)), dma((2,)), dma((6,)), dma((6,)), dma((3,)), dma((3,)),
        ],
        compiler_params=pltpu.CompilerParams(
            collective_id=0 if remote else None,
            has_side_effects=remote,
            vmem_limit_bytes=60 * 1024 * 1024,
        ),
        cost_estimate=pl.CostEstimate(flops=11_000_000_000, bytes_accessed=13_000_000, transcendentals=6_000_000),
        name="window_pair",
    )(images, labels.T, head_scale, cross_scale, *big)


def solution(mesh):
    placed = (P(None, "row", "col", None), P("row", "col")) + (P(),) * 10
    body = functools.partial(device_program, mesh.shape["row"], mesh.shape["col"], True)
    return jax.shard_map(
        body, mesh=mesh, in_specs=placed, out_specs=P("row", "col", None), check_vma=False
    )
```

```python
import functools
import math

import jax
import jax.numpy as jnp
from jax import lax
from jax.experimental import pallas as pl
from jax.experimental.pallas import tpu as pltpu
from jax.sharding import PartitionSpec as P

WIN = 8
SHIFT = 4
HEADS = 16
C = 512
CELL = SHIFT * SHIFT
EPS = 1e-5
LOG2E = math.log2(math.e)
BF = jnp.bfloat16
F32 = jnp.float32
MESH = pl.DeviceIdType.MESH


def dot(a, b):
    return jnp.dot(a, b, preferred_element_type=F32)


def dot_t(a, b):
    return lax.dot_general(a, b, (((1,), (1,)), ((), ())), preferred_element_type=F32)


def iota(shape, dim):
    return lax.broadcasted_iota(jnp.int32, shape, dim)


def norm_rows(v):
    mean = jnp.sum(v, axis=-1, keepdims=True) * (1.0 / C)
    centre = v - mean
    spread = jnp.sum(centre * centre, axis=-1, keepdims=True) * (1.0 / C)
    return centre * lax.rsqrt(spread + EPS)


def pieces(count, step=64):
    return [slice(at, min(at + step, count)) for at in range(0, count, step)]


def gelu_twice(v):
    k = math.sqrt(2.0 / math.pi)
    inner = v * (k + (k * 0.044715) * (v * v))
    return v * (1.0 + jnp.tanh(inner))


BLOCK = [(d, a, 0) for d in range(2) for a in range(3)]
BLOCK += [(d, a, 1) for d in range(2) for a in range(3)]
BLOCK += [(d, 3, b) for d in range(2) for b in range(2)]
NEAR, RIGHT, BELOW = (0, 3, 6), (6, 9, 12), (12, 14, 16)
CROSS = [(1, 1), (2, 1), (3, 1), (1, 0), (2, 0), (3, 0), (0, 0), (0, 1)]
CROSS_NEAR, CROSS_FAR = range(3), range(3, 8)


def cell_rows():
    block, cross = [], []
    for n, (d, a, b) in enumerate(BLOCK):
        for u in range(2):
            for v in range(2):
                block.append(((d, 2 * a + 1 + u, 2 * b + 1 + v), 64 * n + 32 * u + 16 * v))
    for n, (a, b) in enumerate(CROSS):
        for d in range(2):
            for u in range(2):
                for v in range(2):
                    cross.append(((d, 2 * a + u, 2 * b + v), 128 * n + 64 * d + 32 * u + 16 * v))
    return block, cross


def kernel(
    rows, cols, remote,
    img, lab_h, hs, cs, wqkv_h, wp_h, wu_h, wd_h, cqkv_h, cp_h, du_h, dd_h,
    out,
    im, lab, wqkv, wp, wu, wd, cqkv, cp, du, dd,
    xc, gc, sc, perm, bd, ones4, scale_s, qkv_s, att_s, hid_s, first_s, ct_s, ch_s,
    im_sem, lab_sem, w_sem, send1, recv1, send2, recv2,
):
    me_r = lax.axis_index("row") if remote else 0
    me_c = lax.axis_index("col") if remote else 0
    up, down = lax.rem(me_r + rows - 1, rows), lax.rem(me_r + 1, rows)
    left, right = lax.rem(me_c + cols - 1, cols), lax.rem(me_c + 1, cols)

    early = lax.rem(me_c, cols // 2) == 0

    weights = [
        (wqkv_h, wqkv), (wp_h, wp), (wu_h, wu), (wd_h, wd),
        (cqkv_h, cqkv), (cp_h, cp), (du_h, du), (dd_h, dd),
    ]
    loads = [pltpu.make_async_copy(s, d, w_sem.at[n]) for n, (s, d) in enumerate(weights)]
    load_im = pltpu.make_async_copy(img, im, im_sem)
    load_im.start()
    load_lab = pltpu.make_async_copy(lab_h, lab, lab_sem)
    load_lab.start()
    loads[0].start()

    if remote:
        barrier = pltpu.get_barrier_semaphore()
        for r, c in ((up, me_c), (down, me_c), (me_r, left), (me_r, right), (up, left), (down, right)):
            pl.semaphore_signal(barrier, inc=1, device_id={"row": r, "col": c}, device_id_type=MESH)

    o = iota((256, 256), 0)
    t = iota((256, 256), 1)
    src = (((o >> 6) * 4 + ((o >> 2) & 3)) * 16) + ((o >> 4) & 3) * 4 + (o & 3)
    perm[...] = jnp.where(src == t, 1.0, 0.0).astype(BF)

    load_im.wait()
    for load in loads[1:4]:
        load.start()
    for d in range(2):
        for b in range(2):
            block = im[d, 16 * b : 16 * b + 16].reshape(256, C)
            cells = dot(perm[...], block).astype(BF)
            xc[d, 4 * b : 4 * b + 4, 0:4] = cells.reshape(4, 4, CELL, C)

    def send(src, dst, n, r, c, sems, rsems):
        return pltpu.make_async_remote_copy(
            src_ref=src, dst_ref=dst, send_sem=sems.at[n], recv_sem=rsems.at[n],
            device_id={"row": r, "col": c}, device_id_type=MESH,
        )

    block_cells, cross_cells = cell_rows()

    def project(ref, cells, w):
        for n in range(6):
            lanes = slice(256 * n, 256 * n + 256)
            for part in cells:
                y = dot(jnp.concatenate([ref[spot] for spot, _ in part], 0), w[:, lanes]).astype(BF)
                for m, (_, row) in enumerate(part):
                    qkv_s[row : row + 16, lanes] = y[16 * m : 16 * m + 16]

    def unit(cells, scale):
        for n in range(4):
            lanes = slice(256 * n, 256 * n + 256)
            for part in cells:
                y = jnp.concatenate([qkv_s[row : row + 16, lanes] for _, row in part], 0)
                factor = lax.rsqrt(jnp.maximum(dot(y * y, bd[...]), 1.0))
                if n < 2:
                    factor = factor * scale[:, lanes]
                y = (y.astype(F32) * factor).astype(BF)
                for m, (_, row) in enumerate(part):
                    qkv_s[row : row + 16, lanes] = y[16 * m : 16 * m + 16]

    def by_date(cells, here):
        return [[c for c in cells if c[0][0] == d and here(c[0]) ] for d in range(2)]

    own_block = by_date(block_cells, lambda c: c[1] < 8 and c[2] < 4)
    right_block = [[c for c in block_cells if c[0][1] < 7 and c[0][2] == 4]]
    below_block = [[c for c in block_cells if c[0][1] == 8 or c[0][1:] == (7, 4)]]
    own_cross = by_date(cross_cells, lambda c: c[1] > 0 and c[2] > 0)
    far_cross = by_date(cross_cells, lambda c: not (c[1] > 0 and c[2] > 0))

    def on(condition):
        return pl.when(condition) if remote else (lambda work: work())

    if remote:
        halo = [
            send(xc.at[:, 1:7, 0], xc.at[:, 1:7, 4], 0, me_r, left, send1, recv1),
            send(xc.at[:, 0, 1:4], xc.at[:, 8, 1:4], 1, up, me_c, send1, recv1),
            send(xc.at[:, 7, 0], xc.at[:, 7, 4], 2, me_r, left, send1, recv1),
            send(xc.at[:, 0, 0], xc.at[:, 8, 4], 3, up, left, send1, recv1),
            send(gc.at[1:8, 0], gc.at[1:8, 4], 4, me_r, left, send1, recv1),
            send(gc.at[0, 1:4], gc.at[8, 1:4], 5, up, me_c, send1, recv1),
            send(gc.at[0, 0], gc.at[8, 4], 6, up, left, send1, recv1),
        ]

        @pl.when(jnp.logical_not(early))
        def _():
            pl.semaphore_wait(barrier, 6)
            for copy in halo[:4]:
                copy.start()

    loads[0].wait()
    project(xc, own_block, wqkv)
    for load in loads[4:]:
        load.start()

    bd[...] = jnp.where((o >> 5) == (t >> 5), 1.0, 0.0).astype(BF)
    o4 = iota((512, 128), 0)
    t4 = iota((512, 128), 1)
    ones4[0] = jnp.where(((o4 >> 6) & 3) == (t4 >> 5), 1.0, 0.0).astype(BF)
    ones4[1] = jnp.where((o4 >> 7) == (t4 >> 5), 1.0, 0.0).astype(BF)
    lane = iota((8, C), 1) >> 5
    for n, ref in ((0, hs), (1, cs)):
        row = jnp.zeros((8, C), F32)
        for h in range(HEADS):
            row = jnp.where(lane == h, ref[h] * LOG2E, row)
        scale_s[n] = row

    unit(own_block, scale_s[0, 0:1])

    load_lab.wait()
    tok = iota((512, 16), 0)
    tc = ((tok >> 4) & 3) * 4 + (tok & 3)
    pick_c = jnp.where(tc == iota((512, 16), 1), 1.0, 0.0).astype(BF)
    tok = iota((512, 32), 0)
    tr = (tok >> 6) * 4 + ((tok >> 2) & 3)
    by_col = dot(pick_c, lab[...].astype(F32).astype(BF))
    picked = jnp.where(tr == iota((512, 32), 1), by_col, 0.0).astype(BF)
    value = dot(picked, jnp.ones((32, 128), BF)).astype(jnp.int32)
    tok = iota((512, 128), 0)
    gr = (tok >> 6) * 4 + ((tok >> 2) & 3) + me_r * 32
    gcol = ((tok >> 4) & 3) * 4 + (tok & 3) + me_c * 16
    code = value * 4 + jnp.where(gr < SHIFT, 2, 0) + jnp.where(gcol < SHIFT, 1, 0)
    onehot = jnp.where(code == iota((512, 128), 1), 1.0, 0.0).astype(BF)
    gc[0:8, 0:4] = onehot.reshape(8, 4, CELL, 128)
    if remote:
        @pl.when(jnp.logical_not(early))
        def _():
            for copy in halo[4:]:
                copy.start()

        back = [
            send(sc.at[:, 1:7, 4], sc.at[:, 1:7, 0], 0, me_r, right, send2, recv2),
            send(sc.at[:, 7, 4], sc.at[:, 7, 0], 1, me_r, right, send2, recv2),
            send(sc.at[:, 8, 1:4], sc.at[:, 0, 1:4], 2, down, me_c, send2, recv2),
            send(sc.at[:, 8, 4], sc.at[:, 0, 0], 3, down, right, send2, recv2),
        ]

    head_of = iota((1, 128), 1) >> 5
    head_mask = [jnp.where(head_of == h, 1.0, 0.0).astype(BF) for h in range(4)]

    def stacked(v):
        return jnp.concatenate([v * head_mask[h] for h in range(4)], 0)

    def attend(base, count, g, ones, mask):
        lanes = slice(128 * g, 128 * g + 128)
        q = qkv_s[base : base + count, lanes]
        k = qkv_s[base : base + count, 512 + 128 * g : 640 + 128 * g]
        v = qkv_s[base : base + count, 1024 + 128 * g : 1152 + 128 * g]
        e = jnp.exp2(dot_t(q, stacked(k))).astype(BF)
        if mask is not None:
            e = e * mask
        o = dot(e, jnp.concatenate([stacked(v), ones], 1))
        att_s[base : base + count, lanes] = (o[:, :128] * pltpu.reciprocal(o[:, 128:], approx=True)).astype(BF)

    def cells_of(ref, d, i, j):
        return [ref[d, i + u, j + v] for u in range(2) for v in range(2)]

    def spot_of(n):
        d, a, b = BLOCK[n]
        return d, 2 * a + 1, 2 * b + 1

    def block_attend(first_n, mid_n, last_n):
        for n in range(first_n, mid_n):
            _, i, j = spot_of(n)
            codes = jnp.concatenate([gc[i + u, j + v] for u in range(2) for v in range(2)], 0)
            mask = dot_t(codes, jnp.concatenate([codes] * 4, 0)).astype(BF)
            for g in range(4):
                for m in (n, n + mid_n - first_n):
                    attend(64 * m, 64, g, ones4[0, 0:256], mask)

    def block_mlp(first_n, mid_n, last_n, waits):
        chains = [(64 * lo, 64 * hi) for lo, hi in ((first_n, mid_n), (mid_n, last_n))]
        if waits:
            loads[1].wait()
        for lo, hi in chains:
            v = dot(att_s[lo:hi], wp[...])
            for row in range(lo, hi, 64):
                res = jnp.concatenate(cells_of(xc, *spot_of(row // 64)), 0)
                first = res.astype(F32) + norm_rows(v[row - lo : row - lo + 64])
                first_s[row : row + 64] = first.astype(BF)
        if waits:
            loads[2].wait()
        for n in range(8):
            lanes = slice(256 * n, 256 * n + 256)
            for lo, hi in chains:
                hid_s[lo:hi, lanes] = gelu_twice(dot(first_s[lo:hi], wu[:, lanes])).astype(BF)
        if waits:
            loads[3].wait()
        for lo, hi in chains:
            v = dot(hid_s[lo:hi], wd[...])
            for row in range(lo, hi, 64):
                d, i, j = spot_of(row // 64)
                first = first_s[row : row + 64].astype(F32)
                second = (first + norm_rows(0.5 * v[row - lo : row - lo + 64])).astype(BF)
                for u in range(2):
                    for v2 in range(2):
                        at = 32 * u + 16 * v2
                        sc[d, i + u, j + v2] = second[at : at + 16]

    def cross(windows):
        for n in windows:
            for g in range(4):
                attend(128 * n, 128, g, ones4[1], None)
        for n in windows:
            a, b = CROSS[n]
            v = dot(att_s[128 * n : 128 * n + 128], cp[...])
            res = [jnp.concatenate(cells_of(sc, d, 2 * a, 2 * b), 0).astype(F32) for d in range(2)]
            past = res[0] + norm_rows(v[0:64])
            ct_s[64 * n : 64 * n + 64] = res[1] + norm_rows(v[64:128]) - past

    def difference(windows):
        lo, hi = 64 * windows[0], 64 * windows[-1] + 64
        operand = ct_s[lo:hi].astype(BF)
        for n in range(4):
            lanes = slice(256 * n, 256 * n + 256)
            hid_s[lo:hi, lanes] = gelu_twice(dot(operand, du[:, lanes])).astype(BF)
        v = dot(hid_s[lo:hi, 0:1024], dd[...])
        for n in windows:
            a, b = CROSS[n]
            change = ct_s[64 * n : 64 * n + 64] + norm_rows(0.5 * v[64 * n - lo : 64 * n - lo + 64])
            ch_s[a, 64 * b : 64 * b + 64] = change.astype(BF)

    block_attend(*NEAR)
    if remote:
        @pl.when(early)
        def _():
            block_mlp(*NEAR, True)
            pl.semaphore_wait(barrier, 6)
            for copy in halo:
                copy.start()

        halo[0].wait_recv()
    project(xc, right_block, wqkv)
    if remote:
        halo[4].wait_recv()
    unit(right_block, scale_s[0, 0:1])
    block_attend(*RIGHT)

    @on(jnp.logical_not(early))
    def _():
        for n in range(1, 4):
            loads[n].wait()

    block_mlp(*RIGHT, False)
    if remote:
        back[0].start()
        for copy in halo[1:4] + halo[5:]:
            copy.wait_recv()
    project(xc, below_block, wqkv)
    unit(below_block, scale_s[0, 0:1])
    block_attend(*BELOW)
    block_mlp(*BELOW, False)
    if remote:
        for copy in back[1:]:
            copy.start()

    @on(jnp.logical_not(early))
    def _():
        block_mlp(*NEAR, False)

    for n in range(4, 8):
        loads[n].wait()
    project(sc, own_cross, cqkv)
    unit(own_cross, scale_s[1, 0:1])
    cross(CROSS_NEAR)
    difference(CROSS_NEAR)
    if remote:
        for copy in back:
            copy.wait_recv()
    project(sc, far_cross, cqkv)
    unit(far_cross, scale_s[1, 0:1])
    cross(CROSS_FAR)
    difference(CROSS_FAR)

    oo = iota((128, 128), 0)
    tt = iota((128, 128), 1)
    r, c = oo >> 4, oo & 15
    spot = (c >> 3) * 64 + (r >> 2) * 32 + ((c >> 2) & 1) * 16 + (r & 3) * 4 + (c & 3)
    order = jnp.where(spot == tt, 1.0, 0.0).astype(BF)
    for band in range(4):
        out[8 * band : 8 * band + 8] = dot(order, ch_s[band]).astype(BF).reshape(8, 16, C)
    if remote:
        for copy in halo + back:
            copy.wait_send()


def device_program(rows, cols, remote, images, labels, qkv_weight, proj_weight, up_weight, down_weight,
                   head_scale, cross_qkv, cross_proj, cross_scale, diff_up, diff_down):
    any_spec = pl.BlockSpec(memory_space=pl.ANY)
    smem = pl.BlockSpec(memory_space=pltpu.SMEM)
    big = [qkv_weight, proj_weight, up_weight, down_weight, cross_qkv, cross_proj, diff_up, diff_down]
    dma = pltpu.SemaphoreType.DMA
    return pl.pallas_call(
        functools.partial(kernel, rows, cols, remote),
        out_shape=pltpu.VMEM((32, 16, C), BF),
        in_specs=[any_spec, any_spec, smem, smem] + [any_spec] * 8,
        out_specs=pl.BlockSpec(memory_space=pltpu.VMEM),
        scratch_shapes=[
            pltpu.VMEM((2, 32, 16, C), BF),
            pltpu.VMEM((16, 32), jnp.int32),
            *[pltpu.VMEM(w.shape, BF) for w in big],
            pltpu.VMEM((2, 9, 5, CELL, C), BF),
            pltpu.VMEM((9, 5, CELL, 128), BF),
            pltpu.VMEM((2, 9, 5, CELL, C), BF),
            pltpu.VMEM((256, 256), BF),
            pltpu.VMEM((256, 256), BF),
            pltpu.VMEM((2, 512, 128), BF),
            pltpu.VMEM((2, 8, C), F32),
            pltpu.VMEM((1024, 3 * C), BF),
            pltpu.VMEM((1024, C), BF),
            pltpu.VMEM((1024, 2048), BF),
            pltpu.VMEM((1024, C), BF),
            pltpu.VMEM((512, C), F32),
            pltpu.VMEM((4, 128, C), BF),
            dma, dma, dma((8,)), dma((7,)), dma((7,)), dma((4,)), dma((4,)),
        ],
        compiler_params=pltpu.CompilerParams(
            collective_id=0 if remote else None,
            has_side_effects=remote,
            vmem_limit_bytes=60 * 1024 * 1024,
        ),
        cost_estimate=pl.CostEstimate(flops=11_000_000_000, bytes_accessed=13_000_000, transcendentals=6_000_000),
        name="window_pair",
    )(images, labels.T, head_scale, cross_scale, *big)


def solution(mesh):
    placed = (P(None, "row", "col", None), P("row", "col")) + (P(),) * 10
    body = functools.partial(device_program, mesh.shape["row"], mesh.shape["col"], True)
    return jax.shard_map(
        body, mesh=mesh, in_specs=placed, out_specs=P("row", "col", None), check_vma=False
    )
```

```python
import functools
import math

import jax
import jax.numpy as jnp
from jax import lax
from jax.experimental import pallas as pl
from jax.experimental.pallas import tpu as pltpu
from jax.sharding import PartitionSpec as P

WIN = 8
SHIFT = 4
HEADS = 16
C = 512
CELL = SHIFT * SHIFT
EPS = 1e-5
LOG2E = math.log2(math.e)
BF = jnp.bfloat16
F32 = jnp.float32
MESH = pl.DeviceIdType.MESH


def dot(a, b):
    return jnp.dot(a, b, preferred_element_type=F32)


def dot_t(a, b):
    return lax.dot_general(a, b, (((1,), (1,)), ((), ())), preferred_element_type=F32)


def iota(shape, dim):
    return lax.broadcasted_iota(jnp.int32, shape, dim)


def norm_rows(v):
    mean = jnp.sum(v, axis=-1, keepdims=True) * (1.0 / C)
    square = jnp.sum(v * v, axis=-1, keepdims=True) * (1.0 / C)
    factor = lax.rsqrt(jnp.maximum(square - mean * mean, 0.0) + EPS)
    return v * factor - mean * factor


def gelu_twice(v):
    k = math.sqrt(2.0 / math.pi)
    inner = v * (k + (k * 0.044715) * (v * v))
    return v * (1.0 + jnp.tanh(inner))


BLOCK = [(d, a, 0) for d in range(2) for a in range(3)]
BLOCK += [(d, a, 1) for d in range(2) for a in range(3)]
BLOCK += [(d, 3, b) for d in range(2) for b in range(2)]
NEAR, RIGHT, BELOW = (0, 3, 6), (6, 9, 12), (12, 14, 16)
CROSS = [(1, 1), (2, 1), (3, 1), (1, 0), (2, 0), (3, 0), (0, 0), (0, 1)]
CROSS_NEAR, CROSS_MID, CROSS_FAR = range(3), range(3, 5), range(5, 8)


def cell_rows():
    block, cross = [], []
    for n, (d, a, b) in enumerate(BLOCK):
        for u in range(2):
            for v in range(2):
                block.append(((d, 2 * a + 1 + u, 2 * b + 1 + v), 64 * n + 32 * u + 16 * v))
    for n, (a, b) in enumerate(CROSS):
        for d in range(2):
            for u in range(2):
                for v in range(2):
                    cross.append(((d, 2 * a + u, 2 * b + v), 128 * n + 64 * d + 32 * u + 16 * v))
    return block, cross


def kernel(
    rows, cols, remote,
    img, lab_h, hs, cs, wqkv_h, wp_h, wu_h, wd_h, cqkv_h, cp_h, du_h, dd_h,
    out,
    im, lab, wqkv, wp, wu, wd, cqkv, cp, du, dd,
    xc, gc, sc, perm, bd, ones4, scale_s, qkv_s, cqkv_s, att_s, hid_s, first_s, ct_s, ch_s,
    im_sem, lab_sem, w_sem, send1, recv1, send2, recv2,
):
    me_r = lax.axis_index("row") if remote else 0
    me_c = lax.axis_index("col") if remote else 0
    up, down = lax.rem(me_r + rows - 1, rows), lax.rem(me_r + 1, rows)
    left, right = lax.rem(me_c + cols - 1, cols), lax.rem(me_c + 1, cols)

    early = lax.rem(me_c, cols // 2) == 0
    near_first = jnp.logical_or(early, lax.rem(me_c, 2) == 1)

    weights = [
        (wqkv_h, wqkv), (wp_h, wp), (wu_h, wu), (wd_h, wd),
        (cqkv_h, cqkv), (cp_h, cp), (du_h, du), (dd_h, dd),
    ]
    loads = [pltpu.make_async_copy(s, d, w_sem.at[n]) for n, (s, d) in enumerate(weights)]
    load_im = pltpu.make_async_copy(img, im, im_sem)
    load_im.start()
    load_lab = pltpu.make_async_copy(lab_h, lab, lab_sem)
    load_lab.start()
    loads[0].start()

    if remote:
        barrier = pltpu.get_barrier_semaphore()
        for r, c in ((up, me_c), (down, me_c), (me_r, left), (me_r, right), (up, left), (down, right)):
            pl.semaphore_signal(barrier, inc=1, device_id={"row": r, "col": c}, device_id_type=MESH)

    o = iota((256, 256), 0)
    t = iota((256, 256), 1)
    src = (((o >> 6) * 4 + ((o >> 2) & 3)) * 16) + ((o >> 4) & 3) * 4 + (o & 3)
    perm[...] = jnp.where(src == t, 1.0, 0.0).astype(BF)

    load_im.wait()
    for load in loads[1:4]:
        load.start()
    for d in range(2):
        for b in range(2):
            block = im[d, 16 * b : 16 * b + 16].reshape(256, C)
            cells = dot(perm[...], block).astype(BF)
            xc[d, 4 * b : 4 * b + 4, 0:4] = cells.reshape(4, 4, CELL, C)

    def send(src, dst, n, r, c, sems, rsems):
        return pltpu.make_async_remote_copy(
            src_ref=src, dst_ref=dst, send_sem=sems.at[n], recv_sem=rsems.at[n],
            device_id={"row": r, "col": c}, device_id_type=MESH,
        )

    block_cells, cross_cells = cell_rows()

    def project(held, ref, cells, w):
        for n in range(6):
            lanes = slice(256 * n, 256 * n + 256)
            for part in cells:
                y = dot(jnp.concatenate([ref[spot] for spot, _ in part], 0), w[:, lanes]).astype(BF)
                for m, (_, row) in enumerate(part):
                    held[row : row + 16, lanes] = y[16 * m : 16 * m + 16]

    def unit(held, cells, scale):
        for n in range(4):
            lanes = slice(256 * n, 256 * n + 256)
            for part in cells:
                y = jnp.concatenate([held[row : row + 16, lanes] for _, row in part], 0)
                factor = lax.rsqrt(jnp.maximum(dot(y * y, bd[...]), 1.0))
                if n < 2:
                    factor = factor * scale[:, lanes]
                y = y * factor.astype(BF)
                for m, (_, row) in enumerate(part):
                    held[row : row + 16, lanes] = y[16 * m : 16 * m + 16]

    def by_date(cells, here):
        return [[c for c in cells if c[0][0] == d and here(c[0]) ] for d in range(2)]

    own_block = by_date(block_cells, lambda c: c[1] < 8 and c[2] < 4)
    right_block = [[c for c in block_cells if c[0][1] < 7 and c[0][2] == 4]]
    below_block = [[c for c in block_cells if c[0][1] == 8 or c[0][1:] == (7, 4)]]
    near_cross = by_date(cross_cells, lambda c: 0 < c[1] < 7 and 0 < c[2] < 3)
    own_cross = [[c for c in cross_cells if min(c[0][1:]) > 0 and not (c[0][1] < 7 and c[0][2] < 3)]]
    mid_cross = [[c for c in cross_cells if 1 < c[0][1] < 6 and c[0][2] == 0]]
    far_cross = [[c for c in cross_cells if c[0][1] == 0 or (c[0][1] in (1, 6, 7) and c[0][2] == 0)]]

    def on(condition):
        return pl.when(condition) if remote else (lambda work: work())

    if remote:
        halo = [
            send(xc.at[0, 1:7, 0], xc.at[0, 1:7, 4], 0, me_r, left, send1, recv1),
            send(xc.at[:, 0, 1:4], xc.at[:, 8, 1:4], 1, up, me_c, send1, recv1),
            send(xc.at[:, 7, 0], xc.at[:, 7, 4], 2, me_r, left, send1, recv1),
            send(xc.at[:, 0, 0], xc.at[:, 8, 4], 3, up, left, send1, recv1),
            send(gc.at[1:8, 0], gc.at[1:8, 4], 4, me_r, left, send1, recv1),
            send(gc.at[0, 1:4], gc.at[8, 1:4], 5, up, me_c, send1, recv1),
            send(gc.at[0, 0], gc.at[8, 4], 6, up, left, send1, recv1),
            send(xc.at[1, 1:7, 0], xc.at[1, 1:7, 4], 7, me_r, left, send1, recv1),
        ]

        @pl.when(jnp.logical_not(early))
        def _():
            pl.semaphore_wait(barrier, 6)
            for n in (0, 7, 1, 2, 3):
                halo[n].start()

    loads[0].wait()
    project(qkv_s, xc, own_block, wqkv)
    for load in loads[4:]:
        load.start()

    bd[...] = jnp.where((o >> 5) == (t >> 5), 1.0, 0.0).astype(BF)
    o4 = iota((512, 128), 0)
    t4 = iota((512, 128), 1)
    ones4[0] = jnp.where(((o4 >> 6) & 3) == (t4 >> 5), 1.0, 0.0).astype(BF)
    ones4[1] = jnp.where((o4 >> 7) == (t4 >> 5), 1.0, 0.0).astype(BF)
    lane = iota((8, C), 1) >> 5
    for n, ref in ((0, hs), (1, cs)):
        row = jnp.zeros((8, C), F32)
        for h in range(HEADS):
            row = jnp.where(lane == h, ref[h] * LOG2E, row)
        scale_s[n] = row

    unit(qkv_s, own_block, scale_s[0, 0:1])

    load_lab.wait()
    tok = iota((512, 16), 0)
    tc = ((tok >> 4) & 3) * 4 + (tok & 3)
    pick_c = jnp.where(tc == iota((512, 16), 1), 1.0, 0.0).astype(BF)
    tok = iota((512, 32), 0)
    tr = (tok >> 6) * 4 + ((tok >> 2) & 3)
    by_col = dot(pick_c, lab[...].astype(F32).astype(BF))
    picked = jnp.where(tr == iota((512, 32), 1), by_col, 0.0).astype(BF)
    value = dot(picked, jnp.ones((32, 128), BF)).astype(jnp.int32)
    tok = iota((512, 128), 0)
    gr = (tok >> 6) * 4 + ((tok >> 2) & 3) + me_r * 32
    gcol = ((tok >> 4) & 3) * 4 + (tok & 3) + me_c * 16
    code = value * 4 + jnp.where(gr < SHIFT, 2, 0) + jnp.where(gcol < SHIFT, 1, 0)
    onehot = jnp.where(code == iota((512, 128), 1), 1.0, 0.0).astype(BF)
    gc[0:8, 0:4] = onehot.reshape(8, 4, CELL, 128)
    if remote:
        @pl.when(jnp.logical_not(early))
        def _():
            for copy in halo[4:7]:
                copy.start()

        back = [
            send(sc.at[:, 1:7, 4], sc.at[:, 1:7, 0], 0, me_r, right, send2, recv2),
            send(sc.at[:, 7, 4], sc.at[:, 7, 0], 1, me_r, right, send2, recv2),
            send(sc.at[:, 8, 1:4], sc.at[:, 0, 1:4], 2, down, me_c, send2, recv2),
            send(sc.at[:, 8, 4], sc.at[:, 0, 0], 3, down, right, send2, recv2),
        ]

    head_of = iota((1, 128), 1) >> 5
    head_mask = [jnp.where(head_of == h, 1.0, 0.0).astype(BF) for h in range(4)]

    def stacked(v):
        return jnp.concatenate([v * head_mask[h] for h in range(4)], 0)

    def attend(held, base, count, g, ones, mask):
        lanes = slice(128 * g, 128 * g + 128)
        q = held[base : base + count, lanes]
        k = held[base : base + count, 512 + 128 * g : 640 + 128 * g]
        v = held[base : base + count, 1024 + 128 * g : 1152 + 128 * g]
        e = jnp.exp2(dot_t(q, stacked(k))).astype(BF)
        if mask is not None:
            e = e * mask
        o = dot(e, jnp.concatenate([stacked(v), ones], 1))
        att_s[base : base + count, lanes] = (o[:, :128] * pltpu.reciprocal(o[:, 128:], approx=True)).astype(BF)

    def cells_of(ref, d, i, j):
        return [ref[d, i + u, j + v] for u in range(2) for v in range(2)]

    def spot_of(n):
        d, a, b = BLOCK[n]
        return d, 2 * a + 1, 2 * b + 1

    def block_attend(first_n, mid_n, last_n):
        for n in range(first_n, mid_n):
            _, i, j = spot_of(n)
            codes = jnp.concatenate([gc[i + u, j + v] for u in range(2) for v in range(2)], 0)
            mask = dot_t(codes, jnp.concatenate([codes] * 4, 0)).astype(BF)
            for g in range(4):
                for m in (n, n + mid_n - first_n):
                    attend(qkv_s, 64 * m, 64, g, ones4[0, 0:256], mask)

    def block_mlp(first_n, mid_n, last_n, waits):
        chains = [(64 * lo, 64 * hi) for lo, hi in ((first_n, mid_n), (mid_n, last_n))]
        if waits:
            loads[1].wait()
        for lo, hi in chains:
            v = dot(att_s[lo:hi], wp[...])
            for row in range(lo, hi, 64):
                res = jnp.concatenate(cells_of(xc, *spot_of(row // 64)), 0)
                first = res.astype(F32) + norm_rows(v[row - lo : row - lo + 64])
                first_s[row : row + 64] = first.astype(BF)
        if waits:
            loads[2].wait()
        for n in range(8):
            lanes = slice(256 * n, 256 * n + 256)
            for lo, hi in chains:
                hid_s[lo:hi, lanes] = gelu_twice(dot(first_s[lo:hi], wu[:, lanes])).astype(BF)
        if waits:
            loads[3].wait()
        for lo, hi in chains:
            v = dot(hid_s[lo:hi], wd[...])
            for row in range(lo, hi, 64):
                d, i, j = spot_of(row // 64)
                first = first_s[row : row + 64].astype(F32)
                second = (first + norm_rows(0.5 * v[row - lo : row - lo + 64])).astype(BF)
                for u in range(2):
                    for v2 in range(2):
                        at = 32 * u + 16 * v2
                        sc[d, i + u, j + v2] = second[at : at + 16]

    def cross(windows):
        for n in windows:
            for g in range(4):
                attend(cqkv_s, 128 * n, 128, g, ones4[1], None)
        for n in windows:
            a, b = CROSS[n]
            v = dot(att_s[128 * n : 128 * n + 128], cp[...])
            res = [jnp.concatenate(cells_of(sc, d, 2 * a, 2 * b), 0).astype(F32) for d in range(2)]
            past = res[0] + norm_rows(v[0:64])
            ct_s[64 * n : 64 * n + 64] = res[1] + norm_rows(v[64:128]) - past

    def difference(windows):
        lo, hi = 64 * windows[0], 64 * windows[-1] + 64
        operand = ct_s[lo:hi].astype(BF)
        for n in range(4):
            lanes = slice(256 * n, 256 * n + 256)
            hid_s[lo:hi, lanes] = gelu_twice(dot(operand, du[:, lanes])).astype(BF)
        v = dot(hid_s[lo:hi, 0:1024], dd[...])
        for n in windows:
            a, b = CROSS[n]
            change = ct_s[64 * n : 64 * n + 64] + norm_rows(0.5 * v[64 * n - lo : 64 * n - lo + 64])
            ch_s[a, 64 * b : 64 * b + 64] = change.astype(BF)

    def near_windows(waits):
        block_mlp(*NEAR, waits)
        loads[4].wait()
        project(cqkv_s, sc, near_cross, cqkv)
        unit(cqkv_s, near_cross, scale_s[1, 0:1])

    block_attend(*NEAR)
    if remote:
        @pl.when(early)
        def _():
            pl.semaphore_wait(barrier, 6)
            for n in (0, 4, 7, 1, 2, 3, 5, 6):
                halo[n].start()

        @pl.when(near_first)
        def _():
            near_windows(True)

    if remote:
        halo[0].wait_recv()
        halo[7].wait_recv()
    project(qkv_s, xc, right_block, wqkv)
    if remote:
        halo[4].wait_recv()
    unit(qkv_s, right_block, scale_s[0, 0:1])
    block_attend(*RIGHT)

    @on(jnp.logical_not(near_first))
    def _():
        for n in range(1, 4):
            loads[n].wait()

    block_mlp(*RIGHT, False)
    if remote:
        back[0].start()
        for copy in halo[1:4] + halo[5:7]:
            copy.wait_recv()
    project(qkv_s, xc, below_block, wqkv)
    unit(qkv_s, below_block, scale_s[0, 0:1])
    block_attend(*BELOW)
    block_mlp(*BELOW, False)
    if remote:
        for copy in back[1:]:
            copy.start()

    @on(jnp.logical_not(near_first))
    def _():
        near_windows(False)

    for n in range(5, 8):
        loads[n].wait()
    project(cqkv_s, sc, own_cross, cqkv)
    unit(cqkv_s, own_cross, scale_s[1, 0:1])
    cross(CROSS_NEAR)
    if remote:
        back[0].wait_recv()
    project(cqkv_s, sc, mid_cross, cqkv)
    unit(cqkv_s, mid_cross, scale_s[1, 0:1])
    cross(CROSS_MID)
    difference(range(5))
    if remote:
        for copy in back[1:]:
            copy.wait_recv()
    project(cqkv_s, sc, far_cross, cqkv)
    unit(cqkv_s, far_cross, scale_s[1, 0:1])
    cross(CROSS_FAR)
    difference(CROSS_FAR)

    oo = iota((128, 128), 0)
    tt = iota((128, 128), 1)
    r, c = oo >> 4, oo & 15
    spot = (c >> 3) * 64 + (r >> 2) * 32 + ((c >> 2) & 1) * 16 + (r & 3) * 4 + (c & 3)
    order = jnp.where(spot == tt, 1.0, 0.0).astype(BF)
    for band in range(4):
        out[8 * band : 8 * band + 8] = dot(order, ch_s[band]).astype(BF).reshape(8, 16, C)
    if remote:
        for copy in halo + back:
            copy.wait_send()


def device_program(rows, cols, remote, images, labels, qkv_weight, proj_weight, up_weight, down_weight,
                   head_scale, cross_qkv, cross_proj, cross_scale, diff_up, diff_down):
    any_spec = pl.BlockSpec(memory_space=pl.ANY)
    smem = pl.BlockSpec(memory_space=pltpu.SMEM)
    big = [qkv_weight, proj_weight, up_weight, down_weight, cross_qkv, cross_proj, diff_up, diff_down]
    dma = pltpu.SemaphoreType.DMA
    return pl.pallas_call(
        functools.partial(kernel, rows, cols, remote),
        out_shape=pltpu.VMEM((32, 16, C), BF),
        in_specs=[any_spec, any_spec, smem, smem] + [any_spec] * 8,
        out_specs=pl.BlockSpec(memory_space=pltpu.VMEM),
        scratch_shapes=[
            pltpu.VMEM((2, 32, 16, C), BF),
            pltpu.VMEM((16, 32), jnp.int32),
            *[pltpu.VMEM(w.shape, BF) for w in big],
            pltpu.VMEM((2, 9, 5, CELL, C), BF),
            pltpu.VMEM((9, 5, CELL, 128), BF),
            pltpu.VMEM((2, 9, 5, CELL, C), BF),
            pltpu.VMEM((256, 256), BF),
            pltpu.VMEM((256, 256), BF),
            pltpu.VMEM((2, 512, 128), BF),
            pltpu.VMEM((2, 8, C), F32),
            pltpu.VMEM((1024, 3 * C), BF),
            pltpu.VMEM((1024, 3 * C), BF),
            pltpu.VMEM((1024, C), BF),
            pltpu.VMEM((1024, 2048), BF),
            pltpu.VMEM((1024, C), BF),
            pltpu.VMEM((512, C), F32),
            pltpu.VMEM((4, 128, C), BF),
            dma, dma, dma((8,)), dma((8,)), dma((8,)), dma((4,)), dma((4,)),
        ],
        compiler_params=pltpu.CompilerParams(
            collective_id=0 if remote else None,
            has_side_effects=remote,
            vmem_limit_bytes=60 * 1024 * 1024,
        ),
        cost_estimate=pl.CostEstimate(flops=11_000_000_000, bytes_accessed=13_000_000, transcendentals=6_000_000),
        name="window_pair",
    )(images, labels.T, head_scale, cross_scale, *big)


def solution(mesh):
    placed = (P(None, "row", "col", None), P("row", "col")) + (P(),) * 10
    body = functools.partial(device_program, mesh.shape["row"], mesh.shape["col"], True)
    return jax.shard_map(
        body, mesh=mesh, in_specs=placed, out_specs=P("row", "col", None), check_vma=False
    )
```

```python
import functools
import math

import jax
import jax.numpy as jnp
from jax import lax
from jax.experimental import pallas as pl
from jax.experimental.pallas import tpu as pltpu
from jax.sharding import PartitionSpec as P

WIN = 8
SHIFT = 4
HEADS = 16
C = 512
CELL = SHIFT * SHIFT
EPS = 1e-5
LOG2E = math.log2(math.e)
BF = jnp.bfloat16
F32 = jnp.float32
MESH = pl.DeviceIdType.MESH


def dot(a, b):
    return jnp.dot(a, b, preferred_element_type=F32)


def dot_t(a, b):
    return lax.dot_general(a, b, (((1,), (1,)), ((), ())), preferred_element_type=F32)


def iota(shape, dim):
    return lax.broadcasted_iota(jnp.int32, shape, dim)


def norm_rows(v):
    mean = jnp.sum(v, axis=-1, keepdims=True) * (1.0 / C)
    square = jnp.sum(v * v, axis=-1, keepdims=True) * (1.0 / C)
    factor = lax.rsqrt(jnp.maximum(square - mean * mean, 0.0) + EPS)
    return v * factor - mean * factor


def gelu_twice(v):
    k = math.sqrt(2.0 / math.pi)
    inner = v * (k + (k * 0.044715) * (v * v))
    return v * (1.0 + jnp.tanh(inner))


BLOCK = [(d, a, 0) for d in range(2) for a in range(3)]
BLOCK += [(d, a, 1) for d in range(2) for a in range(3)]
BLOCK += [(d, 3, b) for d in range(2) for b in range(2)]
NEAR, RIGHT, BELOW = (0, 3, 6), (6, 9, 12), (12, 14, 16)
CROSS = [(1, 1), (2, 1), (3, 1), (1, 0), (2, 0), (3, 0), (0, 0), (0, 1)]
CROSS_NEAR, CROSS_MID, CROSS_FAR = range(3), range(3, 5), range(5, 8)


def cell_rows():
    block, cross = [], []
    for n, (d, a, b) in enumerate(BLOCK):
        for u in range(2):
            for v in range(2):
                block.append(((d, 2 * a + 1 + u, 2 * b + 1 + v), 64 * n + 32 * u + 16 * v))
    for n, (a, b) in enumerate(CROSS):
        for d in range(2):
            for u in range(2):
                for v in range(2):
                    cross.append(((d, 2 * a + u, 2 * b + v), 128 * n + 64 * d + 32 * u + 16 * v))
    return block, cross


def kernel(
    rows, cols, remote,
    img, lab_h, hs, cs, wqkv_h, wp_h, wu_h, wd_h, cqkv_h, cp_h, du_h, dd_h,
    out,
    im, lab, wqkv, wp, wu, wd, cqkv, cp, du, dd,
    xc, gc, sc, perm, bd, ones4, scale_s, qkv_s, cqkv_s, att_s, hid_s, first_s, ct_s, ch_s,
    im_sem, lab_sem, w_sem, send1, recv1, send2, recv2,
):
    me_r = lax.axis_index("row") if remote else 0
    me_c = lax.axis_index("col") if remote else 0
    up, down = lax.rem(me_r + rows - 1, rows), lax.rem(me_r + 1, rows)
    left, right = lax.rem(me_c + cols - 1, cols), lax.rem(me_c + 1, cols)

    early = lax.rem(me_c, cols // 2) == 0
    near_first = jnp.logical_or(early, lax.rem(me_c, 2) == 1)

    weights = [
        (wqkv_h, wqkv), (wp_h, wp), (wu_h, wu), (wd_h, wd),
        (cqkv_h, cqkv), (cp_h, cp), (du_h, du), (dd_h, dd),
    ]
    loads = [pltpu.make_async_copy(s, d, w_sem.at[n]) for n, (s, d) in enumerate(weights)]
    load_im = pltpu.make_async_copy(img, im, im_sem)
    load_im.start()
    load_lab = pltpu.make_async_copy(lab_h, lab, lab_sem)
    load_lab.start()

    if remote:
        barrier = pltpu.get_barrier_semaphore()
        for r, c in ((up, me_c), (down, me_c), (me_r, left), (me_r, right), (up, left), (down, right)):
            pl.semaphore_signal(barrier, inc=1, device_id={"row": r, "col": c}, device_id_type=MESH)

    o = iota((256, 256), 0)
    t = iota((256, 256), 1)
    src = (((o >> 6) * 4 + ((o >> 2) & 3)) * 16) + ((o >> 4) & 3) * 4 + (o & 3)
    perm[...] = jnp.where(src == t, 1.0, 0.0).astype(BF)

    load_im.wait()
    for load in loads[0:4]:
        load.start()
    for d in range(2):
        for b in range(2):
            block = im[d, 16 * b : 16 * b + 16].reshape(256, C)
            cells = dot(perm[...], block).astype(BF)
            xc[d, 4 * b : 4 * b + 4, 0:4] = cells.reshape(4, 4, CELL, C)

    def send(src, dst, n, r, c, sems, rsems):
        return pltpu.make_async_remote_copy(
            src_ref=src, dst_ref=dst, send_sem=sems.at[n], recv_sem=rsems.at[n],
            device_id={"row": r, "col": c}, device_id_type=MESH,
        )

    block_cells, cross_cells = cell_rows()

    def project(held, ref, cells, w):
        for n in range(6):
            lanes = slice(256 * n, 256 * n + 256)
            for part in cells:
                y = dot(jnp.concatenate([ref[spot] for spot, _ in part], 0), w[:, lanes]).astype(BF)
                for m, (_, row) in enumerate(part):
                    held[row : row + 16, lanes] = y[16 * m : 16 * m + 16]

    def unit(held, cells, scale):
        for n in range(4):
            lanes = slice(256 * n, 256 * n + 256)
            for part in cells:
                y = jnp.concatenate([held[row : row + 16, lanes] for _, row in part], 0)
                factor = lax.rsqrt(jnp.maximum(dot(y * y, bd[...]), 1.0))
                if n < 2:
                    factor = factor * scale[:, lanes]
                y = y * factor.astype(BF)
                for m, (_, row) in enumerate(part):
                    held[row : row + 16, lanes] = y[16 * m : 16 * m + 16]

    def by_date(cells, here):
        return [[c for c in cells if c[0][0] == d and here(c[0]) ] for d in range(2)]

    own_block = by_date(block_cells, lambda c: c[1] < 8 and c[2] < 4)
    right_block = [[c for c in block_cells if c[0][1] < 7 and c[0][2] == 4]]
    below_block = [[c for c in block_cells if c[0][1] == 8 or c[0][1:] == (7, 4)]]
    near_cross = by_date(cross_cells, lambda c: 0 < c[1] < 7 and 0 < c[2] < 3)
    own_cross = [[c for c in cross_cells if min(c[0][1:]) > 0 and not (c[0][1] < 7 and c[0][2] < 3)]]
    mid_cross = [[c for c in cross_cells if 1 < c[0][1] < 6 and c[0][2] == 0]]
    far_cross = [[c for c in cross_cells if c[0][1] == 0 or (c[0][1] in (1, 6, 7) and c[0][2] == 0)]]

    def on(condition):
        return pl.when(condition) if remote else (lambda work: work())

    if remote:
        halo = [
            send(xc.at[0, 1:7, 0], xc.at[0, 1:7, 4], 0, me_r, left, send1, recv1),
            send(xc.at[:, 0, 1:4], xc.at[:, 8, 1:4], 1, up, me_c, send1, recv1),
            send(xc.at[:, 7, 0], xc.at[:, 7, 4], 2, me_r, left, send1, recv1),
            send(xc.at[:, 0, 0], xc.at[:, 8, 4], 3, up, left, send1, recv1),
            send(gc.at[1:8, 0], gc.at[1:8, 4], 4, me_r, left, send1, recv1),
            send(gc.at[0, 1:4], gc.at[8, 1:4], 5, up, me_c, send1, recv1),
            send(gc.at[0, 0], gc.at[8, 4], 6, up, left, send1, recv1),
            send(xc.at[1, 1:7, 0], xc.at[1, 1:7, 4], 7, me_r, left, send1, recv1),
        ]

        @pl.when(jnp.logical_not(early))
        def _():
            pl.semaphore_wait(barrier, 6)
            for n in (0, 7, 1, 2, 3):
                halo[n].start()

    load_lab.wait()
    tok = iota((512, 16), 0)
    tc = ((tok >> 4) & 3) * 4 + (tok & 3)
    pick_c = jnp.where(tc == iota((512, 16), 1), 1.0, 0.0).astype(BF)
    tok = iota((512, 32), 0)
    tr = (tok >> 6) * 4 + ((tok >> 2) & 3)
    by_col = dot(pick_c, lab[...].astype(F32).astype(BF))
    picked = jnp.where(tr == iota((512, 32), 1), by_col, 0.0).astype(BF)
    value = dot(picked, jnp.ones((32, 128), BF)).astype(jnp.int32)
    tok = iota((512, 128), 0)
    gr = (tok >> 6) * 4 + ((tok >> 2) & 3) + me_r * 32
    gcol = ((tok >> 4) & 3) * 4 + (tok & 3) + me_c * 16
    code = value * 4 + jnp.where(gr < SHIFT, 2, 0) + jnp.where(gcol < SHIFT, 1, 0)
    onehot = jnp.where(code == iota((512, 128), 1), 1.0, 0.0).astype(BF)
    gc[0:8, 0:4] = onehot.reshape(8, 4, CELL, 128)
    if remote:
        @pl.when(jnp.logical_not(early))
        def _():
            for copy in halo[4:7]:
                copy.start()

    loads[0].wait()
    project(qkv_s, xc, own_block, wqkv)
    for load in loads[4:]:
        load.start()

    bd[...] = jnp.where((o >> 5) == (t >> 5), 1.0, 0.0).astype(BF)
    o4 = iota((512, 128), 0)
    t4 = iota((512, 128), 1)
    ones4[0] = jnp.where(((o4 >> 6) & 3) == (t4 >> 5), 1.0, 0.0).astype(BF)
    ones4[1] = jnp.where((o4 >> 7) == (t4 >> 5), 1.0, 0.0).astype(BF)
    lane = iota((8, C), 1) >> 5
    for n, ref in ((0, hs), (1, cs)):
        row = jnp.zeros((8, C), F32)
        for h in range(HEADS):
            row = jnp.where(lane == h, ref[h] * LOG2E, row)
        scale_s[n] = row

    unit(qkv_s, own_block, scale_s[0, 0:1])


    if remote:
        back = [
            send(sc.at[:, 1:7, 4], sc.at[:, 1:7, 0], 0, me_r, right, send2, recv2),
            send(sc.at[:, 7, 4], sc.at[:, 7, 0], 1, me_r, right, send2, recv2),
            send(sc.at[:, 8, 1:4], sc.at[:, 0, 1:4], 2, down, me_c, send2, recv2),
            send(sc.at[:, 8, 4], sc.at[:, 0, 0], 3, down, right, send2, recv2),
        ]

    head_of = iota((1, 128), 1) >> 5
    head_mask = [jnp.where(head_of == h, 1.0, 0.0).astype(BF) for h in range(4)]

    def stacked(v):
        return jnp.concatenate([v * head_mask[h] for h in range(4)], 0)

    def attend(held, base, count, g, ones, mask):
        lanes = slice(128 * g, 128 * g + 128)
        q = held[base : base + count, lanes]
        k = held[base : base + count, 512 + 128 * g : 640 + 128 * g]
        v = held[base : base + count, 1024 + 128 * g : 1152 + 128 * g]
        e = jnp.exp2(dot_t(q, stacked(k))).astype(BF)
        if mask is not None:
            e = e * mask
        o = dot(e, jnp.concatenate([stacked(v), ones], 1))
        att_s[base : base + count, lanes] = (o[:, :128] * pltpu.reciprocal(o[:, 128:], approx=True)).astype(BF)

    def cells_of(ref, d, i, j):
        return [ref[d, i + u, j + v] for u in range(2) for v in range(2)]

    def spot_of(n):
        d, a, b = BLOCK[n]
        return d, 2 * a + 1, 2 * b + 1

    def block_attend(first_n, mid_n, last_n):
        for n in range(first_n, mid_n):
            _, i, j = spot_of(n)
            codes = jnp.concatenate([gc[i + u, j + v] for u in range(2) for v in range(2)], 0)
            mask = dot_t(codes, jnp.concatenate([codes] * 4, 0)).astype(BF)
            for g in range(4):
                for m in (n, n + mid_n - first_n):
                    attend(qkv_s, 64 * m, 64, g, ones4[0, 0:256], mask)

    def block_mlp(first_n, mid_n, last_n, waits):
        chains = [(64 * lo, 64 * hi) for lo, hi in ((first_n, mid_n), (mid_n, last_n))]
        if waits:
            loads[1].wait()
        for lo, hi in chains:
            v = dot(att_s[lo:hi], wp[...])
            for row in range(lo, hi, 64):
                res = jnp.concatenate(cells_of(xc, *spot_of(row // 64)), 0)
                first = res.astype(F32) + norm_rows(v[row - lo : row - lo + 64])
                first_s[row : row + 64] = first.astype(BF)
        if waits:
            loads[2].wait()
        for n in range(8):
            lanes = slice(256 * n, 256 * n + 256)
            for lo, hi in chains:
                hid_s[lo:hi, lanes] = gelu_twice(dot(first_s[lo:hi], wu[:, lanes])).astype(BF)
        if waits:
            loads[3].wait()
        for lo, hi in chains:
            v = dot(hid_s[lo:hi], wd[...])
            for row in range(lo, hi, 64):
                d, i, j = spot_of(row // 64)
                first = first_s[row : row + 64].astype(F32)
                second = (first + norm_rows(0.5 * v[row - lo : row - lo + 64])).astype(BF)
                for u in range(2):
                    for v2 in range(2):
                        at = 32 * u + 16 * v2
                        sc[d, i + u, j + v2] = second[at : at + 16]

    def cross(windows):
        for n in windows:
            for g in range(4):
                attend(cqkv_s, 128 * n, 128, g, ones4[1], None)
        for n in windows:
            a, b = CROSS[n]
            v = dot(att_s[128 * n : 128 * n + 128], cp[...])
            res = [jnp.concatenate(cells_of(sc, d, 2 * a, 2 * b), 0).astype(F32) for d in range(2)]
            past = res[0] + norm_rows(v[0:64])
            ct_s[64 * n : 64 * n + 64] = res[1] + norm_rows(v[64:128]) - past

    def difference(windows):
        lo, hi = 64 * windows[0], 64 * windows[-1] + 64
        operand = ct_s[lo:hi].astype(BF)
        for n in range(4):
            lanes = slice(256 * n, 256 * n + 256)
            hid_s[lo:hi, lanes] = gelu_twice(dot(operand, du[:, lanes])).astype(BF)
        v = dot(hid_s[lo:hi, 0:1024], dd[...])
        for n in windows:
            a, b = CROSS[n]
            change = ct_s[64 * n : 64 * n + 64] + norm_rows(0.5 * v[64 * n - lo : 64 * n - lo + 64])
            ch_s[a, 64 * b : 64 * b + 64] = change.astype(BF)

    def near_windows(waits):
        block_mlp(*NEAR, waits)
        loads[4].wait()
        project(cqkv_s, sc, near_cross, cqkv)
        unit(cqkv_s, near_cross, scale_s[1, 0:1])

    block_attend(*NEAR)
    if remote:
        @pl.when(early)
        def _():
            pl.semaphore_wait(barrier, 6)
            for n in (0, 4, 7, 1, 2, 3, 5, 6):
                halo[n].start()

        @pl.when(near_first)
        def _():
            near_windows(True)

    if remote:
        halo[0].wait_recv()
        halo[7].wait_recv()
    project(qkv_s, xc, right_block, wqkv)
    if remote:
        halo[4].wait_recv()
    unit(qkv_s, right_block, scale_s[0, 0:1])
    block_attend(*RIGHT)

    @on(jnp.logical_not(near_first))
    def _():
        for n in range(1, 4):
            loads[n].wait()

    block_mlp(*RIGHT, False)
    if remote:
        back[0].start()
        for copy in halo[1:4] + halo[5:7]:
            copy.wait_recv()
    project(qkv_s, xc, below_block, wqkv)
    unit(qkv_s, below_block, scale_s[0, 0:1])
    block_attend(*BELOW)
    block_mlp(*BELOW, False)
    if remote:
        for copy in back[1:]:
            copy.start()

    @on(jnp.logical_not(near_first))
    def _():
        near_windows(False)

    for n in range(5, 8):
        loads[n].wait()
    project(cqkv_s, sc, own_cross, cqkv)
    unit(cqkv_s, own_cross, scale_s[1, 0:1])
    cross(CROSS_NEAR)
    if remote:
        back[0].wait_recv()
    project(cqkv_s, sc, mid_cross, cqkv)
    unit(cqkv_s, mid_cross, scale_s[1, 0:1])
    cross(CROSS_MID)
    difference(range(5))
    if remote:
        for copy in back[1:]:
            copy.wait_recv()
    project(cqkv_s, sc, far_cross, cqkv)
    unit(cqkv_s, far_cross, scale_s[1, 0:1])
    cross(CROSS_FAR)
    difference(CROSS_FAR)

    oo = iota((128, 128), 0)
    tt = iota((128, 128), 1)
    r, c = oo >> 4, oo & 15
    spot = (c >> 3) * 64 + (r >> 2) * 32 + ((c >> 2) & 1) * 16 + (r & 3) * 4 + (c & 3)
    order = jnp.where(spot == tt, 1.0, 0.0).astype(BF)
    for band in range(4):
        out[8 * band : 8 * band + 8] = dot(order, ch_s[band]).astype(BF).reshape(8, 16, C)
    if remote:
        for copy in halo + back:
            copy.wait_send()


def device_program(rows, cols, remote, images, labels, qkv_weight, proj_weight, up_weight, down_weight,
                   head_scale, cross_qkv, cross_proj, cross_scale, diff_up, diff_down):
    any_spec = pl.BlockSpec(memory_space=pl.ANY)
    smem = pl.BlockSpec(memory_space=pltpu.SMEM)
    big = [qkv_weight, proj_weight, up_weight, down_weight, cross_qkv, cross_proj, diff_up, diff_down]
    dma = pltpu.SemaphoreType.DMA
    return pl.pallas_call(
        functools.partial(kernel, rows, cols, remote),
        out_shape=pltpu.VMEM((32, 16, C), BF),
        in_specs=[any_spec, any_spec, smem, smem] + [any_spec] * 8,
        out_specs=pl.BlockSpec(memory_space=pltpu.VMEM),
        scratch_shapes=[
            pltpu.VMEM((2, 32, 16, C), BF),
            pltpu.VMEM((16, 32), jnp.int32),
            *[pltpu.VMEM(w.shape, BF) for w in big],
            pltpu.VMEM((2, 9, 5, CELL, C), BF),
            pltpu.VMEM((9, 5, CELL, 128), BF),
            pltpu.VMEM((2, 9, 5, CELL, C), BF),
            pltpu.VMEM((256, 256), BF),
            pltpu.VMEM((256, 256), BF),
            pltpu.VMEM((2, 512, 128), BF),
            pltpu.VMEM((2, 8, C), F32),
            pltpu.VMEM((1024, 3 * C), BF),
            pltpu.VMEM((1024, 3 * C), BF),
            pltpu.VMEM((1024, C), BF),
            pltpu.VMEM((1024, 2048), BF),
            pltpu.VMEM((1024, C), BF),
            pltpu.VMEM((512, C), F32),
            pltpu.VMEM((4, 128, C), BF),
            dma, dma, dma((8,)), dma((8,)), dma((8,)), dma((4,)), dma((4,)),
        ],
        compiler_params=pltpu.CompilerParams(
            collective_id=0 if remote else None,
            has_side_effects=remote,
            vmem_limit_bytes=60 * 1024 * 1024,
        ),
        cost_estimate=pl.CostEstimate(flops=11_000_000_000, bytes_accessed=13_000_000, transcendentals=6_000_000),
        name="window_pair",
    )(images, labels.T, head_scale, cross_scale, *big)


def solution(mesh):
    placed = (P(None, "row", "col", None), P("row", "col")) + (P(),) * 10
    body = functools.partial(device_program, mesh.shape["row"], mesh.shape["col"], True)
    return jax.shard_map(
        body, mesh=mesh, in_specs=placed, out_specs=P("row", "col", None), check_vma=False
    )
```
